128 devices in a mesh: shot: 4 (over z_lo, core), sub: 32 (over y, z_hi, x).
Axes of the slice: x: 4, y: 4, z: 4 (z_hi: 2, z_lo: 2; z = z_hi * 2 + z_lo), core: 2. Of those that a mesh axis runs over, the one named last changes fastest.
Arguments:
- courant_tiles: float32 [768, 6, 64, 128], P(('shot', 'sub')), may hold values from 0.2 to 0.44
- tile_place: int32 [64, 12], replicated, may hold values from 0 to 11, each once within a row
- anchors: int32 [4, 2], replicated, may hold values from 0 to 32, as said below
- source_cells: int32 [4, 3], replicated, may hold values from 0 to 383, as said below
- wavelet: float32 [4, 4], P('shot'), may hold values from -6 to 6
- forward_state: float32 [4, 2, 192, 384, 128], P('shot', None, 'sub'), may hold values from -1.75 to 1.75
- adjoint_state: float32 [4, 2, 192, 384, 128], P('shot', None, 'sub'), may hold values from -1.75 to 1.75
- residual: float32 [4, 4, 192, 384], P('shot', None, 'sub'), may hold values from -1.75 to 1.75
Outputs:
- forward_out: float32 [4, 2, 192, 384, 128], P('shot', None, 'sub')
- adjoint_out: float32 [4, 2, 192, 384, 128], P('shot', None, 'sub')
- gradient_tiles: float32 [768, 6, 64, 128], P(('shot', 'sub'))
The draws below stay inside these ranges and needn't reach their ends.
Inputs may be any that keep to these rules, and one draw needn't show every extreme that they name: `anchors`: the first entry is 0 to 32, the second 0 to 6, so that an aperture lies inside the model; some shot's aperture lies at the far end of the first dimension (first entry 32), another's at the anchor. `source_cells`: entries are below 192, 384 and 128 for the three dimensions; some shot's source lies at the aperture's far corner, another's on the plane where the third entry is 0. `tile_place`: each row lists every place 0 to 11 once.
All inputs are finite; a program needn't handle non-finite values.
Results may differ from the reference program's by a relative error of at most 0.00024.
Values sent between devices are 32-bit elements; how exact they have to be, the bound alone decides.
No kernel may reach another device: no remote copies, remote signals or barrier semaphores. Data moves between devices by JAX's collectives and lax.ppermute only.
A program may use at most 128 MiB of HBM per device.

```python
import jax
import jax.numpy as jnp
from jax import lax

CX = 6
TY = 64
AZ = 128
KY = 6
STEPS = 4
AX = 192
AY = 384
GX = 64
GY = 12
CT = 12
SHARE = 3
TILES_DEV = 6
TILES = 768
N_SHOT = 4
N_SUB = 32


def draw_anchors(key, part):
    key = jax.random.fold_in(key, 11)
    keys = jax.random.split(key, 3)
    first = jax.random.randint(keys[0], (N_SHOT,), 0, N_SUB + 1)
    second = jax.random.randint(keys[1], (N_SHOT,), 0, KY + 1)
    chosen = jax.random.randint(keys[2], (), 0, N_SHOT)
    other = (chosen + 1) % N_SHOT
    shots = jnp.arange(N_SHOT, dtype=jnp.int32)
    first = jnp.where(shots == chosen, N_SUB, first)
    first = jnp.where(shots == other, 0, first)
    second = jnp.where(shots == other, 0, second)
    return jnp.stack([first, second], axis=1).astype(jnp.int32)


def draw_source_cells(key, part):
    key = jax.random.fold_in(key, 23)
    keys = jax.random.split(key, 4)
    first = jax.random.randint(keys[0], (N_SHOT,), 0, AX)
    second = jax.random.randint(keys[1], (N_SHOT,), 0, AY)
    third = jax.random.randint(keys[2], (N_SHOT,), 0, AZ)
    chosen = jax.random.randint(keys[3], (), 0, N_SHOT)
    other = (chosen + 1) % N_SHOT
    shots = jnp.arange(N_SHOT, dtype=jnp.int32)
    first = jnp.where(shots == chosen, AX - 1, first)
    second = jnp.where(shots == chosen, AY - 1, second)
    third = jnp.where(shots == chosen, AZ - 1, third)
    third = jnp.where(shots == other, 0, third)
    return jnp.stack([first, second, third], axis=1).astype(jnp.int32)


def level_of(stream_key, dims, cuts, least, top_value):
    level = 1.0
    for position, shards_of in cuts:
        steps = jax.random.uniform(jax.random.fold_in(jax.random.fold_in(stream_key, 6), position), (shards_of,), jnp.float32, least / len(cuts), top_value / len(cuts))
        level = level * jnp.repeat(jnp.exp(steps), dims[position] // shards_of).reshape((-1,) + (1,) * (len(dims) - 1 - position))
    return level


def gaussian(rng, shape, spread, reach, shards=(), kind=jnp.bfloat16):
    loudness = level_of(rng, shape, shards, -0.22, 0.18) if shards else 1.0
    entries = jax.random.normal(rng, shape, jnp.float32) * spread * loudness
    return jnp.minimum(jnp.maximum(entries, -reach), reach).astype(kind)


def setup_inputs(seed: int = 0) -> dict:
    splits = jax.random.split(jax.random.key(seed), 9)
    courant_tiles = jnp.clip(0.2 + 0.24 * jax.random.uniform(splits[0], (TILES, CX, TY, AZ), jnp.float32) ** level_of(splits[0], (TILES, CX, TY, AZ), ((0, 128),), -0.2, 0.2), 0.2, 0.44)
    tile_place = jax.vmap(lambda own: jax.random.permutation(own, CT))(jax.random.split(splits[1], GX)).reshape((GX, CT)).astype(jnp.int32)
    anchors = draw_anchors(jax.random.fold_in(splits[8], 71), 0)
    source_cells = draw_source_cells(jax.random.fold_in(splits[8], 71), 0)
    wavelet = gaussian(splits[4], (N_SHOT, STEPS), 1.0, 6.0, ((0, 4),), jnp.float32)
    forward_state = gaussian(splits[5], (N_SHOT, 2, AX, AY, AZ), 0.3, 1.75, ((0, 4), (2, 32)), jnp.float32)
    adjoint_state = gaussian(splits[6], (N_SHOT, 2, AX, AY, AZ), 0.3, 1.75, ((0, 4), (2, 32)), jnp.float32)
    residual = gaussian(splits[7], (N_SHOT, STEPS, AX, AY), 0.3, 1.75, ((0, 4), (2, 32)), jnp.float32)
    return dict(courant_tiles=courant_tiles, tile_place=tile_place, anchors=anchors, source_cells=source_cells, wavelet=wavelet, forward_state=forward_state, adjoint_state=adjoint_state, residual=residual)


WEIGHTS = (1.6, -0.2, 8.0 / 315.0, -1.0 / 560.0)
CENTER = -205.0 / 72.0 * 3.0


def stencil(padded):
    size_x = padded.shape[0] - 8
    size_y = padded.shape[1] - 8
    size_z = padded.shape[2] - 8
    summed = CENTER * padded[4:4 + size_x, 4:4 + size_y, 4:4 + size_z]
    for distance, weight in enumerate(WEIGHTS, 1):
        summed = summed + weight * (padded[4 + distance:4 + distance + size_x, 4:4 + size_y, 4:4 + size_z] + padded[4 - distance:4 - distance + size_x, 4:4 + size_y, 4:4 + size_z])
    for distance, weight in enumerate(WEIGHTS, 1):
        summed = summed + weight * (padded[4:4 + size_x, 4 + distance:4 + distance + size_y, 4:4 + size_z] + padded[4:4 + size_x, 4 - distance:4 - distance + size_y, 4:4 + size_z])
    for distance, weight in enumerate(WEIGHTS, 1):
        summed = summed + weight * (padded[4:4 + size_x, 4:4 + size_y, 4 + distance:4 + distance + size_z] + padded[4:4 + size_x, 4:4 + size_y, 4 - distance:4 - distance + size_z])
    return summed


def tile_rows(tile_place):
    column = jnp.arange(GX, dtype=jnp.int32)[:, None]
    holder = tile_place // SHARE
    return (holder * N_SUB + column % N_SUB) * TILES_DEV + (column // N_SUB) * SHARE + tile_place % SHARE


def reference(courant_tiles, tile_place, anchors, source_cells, wavelet, forward_state, adjoint_state, residual):
    rows = tile_rows(tile_place).reshape(-1).astype(jnp.int32)
    model = courant_tiles[rows].reshape(GX, GY, CX, TY, AZ).transpose(0, 2, 1, 3, 4).reshape(GX * CX, GY * TY, AZ)
    gradient = jnp.zeros_like(model)
    forward_list = []
    adjoint_list = []
    for shot_index in range(N_SHOT):
        start = ((anchors[shot_index, 0] * CX).astype(jnp.int32), (anchors[shot_index, 1] * TY).astype(jnp.int32), jnp.zeros((), jnp.int32))
        courant = lax.dynamic_slice(model, start, (AX, AY, AZ))
        weight_sq = courant * courant
        previous = forward_state[shot_index, 0]
        current = forward_state[shot_index, 1]
        curvatures = []
        for step in range(STEPS):
            curvature = stencil(jnp.pad(current, 4))
            advanced = 2.0 * current - previous + weight_sq * curvature
            advanced = advanced.at[source_cells[shot_index, 0], source_cells[shot_index, 1], source_cells[shot_index, 2]].add(wavelet[shot_index, step])
            curvatures.append(curvature)
            previous, current = current, advanced
        forward_list.append(jnp.stack([previous, current]))
        adjoint_old = adjoint_state[shot_index, 0]
        adjoint_now = adjoint_state[shot_index, 1]
        kept = []
        for step in range(STEPS):
            kept.append(adjoint_now)
            advanced = 2.0 * adjoint_now - adjoint_old + stencil(jnp.pad(weight_sq * adjoint_now, 4))
            advanced = advanced.at[:, :, 0].add(residual[shot_index, step])
            adjoint_old, adjoint_now = adjoint_now, advanced
        adjoint_list.append(jnp.stack([adjoint_old, adjoint_now]))
        imaging = jnp.zeros((AX, AY, AZ), jnp.float32)
        for step in range(STEPS):
            imaging = imaging + kept[step] * curvatures[STEPS - 1 - step]
        term = 2.0 * courant * imaging
        gradient = lax.dynamic_update_slice(gradient, lax.dynamic_slice(gradient, start, (AX, AY, AZ)) + term, start)
    tiles = gradient.reshape(GX, CX, GY, TY, AZ).transpose(0, 2, 1, 3, 4).reshape(TILES, CX, TY, AZ)
    gradient_tiles = jnp.zeros_like(courant_tiles).at[rows].set(tiles)
    return jnp.stack(forward_list), jnp.stack(adjoint_list), gradient_tiles
```

```python
import functools

import jax
import jax.numpy as jnp
from jax import lax
from jax.experimental import pallas as pl
from jax.experimental.pallas import tpu as pltpu
from jax.sharding import PartitionSpec as P

CX = 6
TY = 64
AZ = 128
KY = 6
AY = KY * TY
STEPS = 4
N_SHOT = 4
N_SUB = 32
SHARE = 3
R = 4
PAD = 8

WEIGHTS = (1.6, -0.2, 8.0 / 315.0, -1.0 / 560.0)
CENTER = -205.0 / 72.0 * 3.0

F32 = jnp.float32
SLAB = (CX, AY, AZ)
HALO = (R, AY, AZ)
BLOCK = pl.BlockSpec((CX, TY, AZ), lambda i, *_: (0, i, 0))
HBLOCK = pl.BlockSpec((R, TY, AZ), lambda i, *_: (0, i, 0))
WHOLE = pl.BlockSpec(SLAB, lambda i, *_: (0, 0, 0))
VMEM = 40 * 1024 * 1024


def sds(shape):
    return jax.ShapeDtypeStruct(shape, F32)


def fill_pad(src, pad):
    @pl.when(pl.program_id(0) == 0)
    def _():
        pad[:, 0:PAD, :] = jnp.zeros((CX, PAD, AZ), F32)
        pad[:, PAD + AY :, :] = jnp.zeros((CX, PAD, AZ), F32)
        pad[:, PAD : PAD + AY, :] = src[...]


def laplacian(x, src, lo, hi, pad):
    base = pl.multiple_of(pl.program_id(0) * TY, TY)

    def plane(k):
        if k < 0:
            return lo[k + R]
        if k >= CX:
            return hi[k - CX]
        return src[k, pl.ds(base, TY), :]

    here = plane(x)
    lane = lax.broadcasted_iota(jnp.int32, (TY, AZ), 1)
    out = CENTER * here
    for r, w in enumerate(WEIGHTS, 1):
        out = out + w * (plane(x + r) + plane(x - r))
    for r, w in enumerate(WEIGHTS, 1):
        out = out + w * (
            pad[x, pl.ds(base + (PAD + r), TY), :] + pad[x, pl.ds(base + (PAD - r), TY), :]
        )
    for r, w in enumerate(WEIGHTS, 1):
        up = jnp.where(lane < AZ - r, pltpu.roll(here, AZ - r, 1), 0.0)
        down = jnp.where(lane >= r, pltpu.roll(here, r, 1), 0.0)
        out = out + w * (up + down)
    return out


def add_source(out, cells, amp, halos):
    col = cells[1] - pl.program_id(0) * TY
    inside = (cells[0] >= 0) & (cells[0] < CX) & (col >= 0) & (col < TY)

    @pl.when(inside)
    def _():
        lane = lax.broadcasted_iota(jnp.int32, (1, 1, AZ), 2)
        x = cells[0]
        row = out[pl.ds(x, 1), pl.ds(col, 1), :]
        out[pl.ds(x, 1), pl.ds(col, 1), :] = row + jnp.where(lane == cells[2], amp, 0.0)

    if halos is not None:
        halos[0][...] = out[0:R]
        halos[1][...] = out[CX - R :]


def lap_kernel(src, lo, hi, lap, pad):
    fill_pad(src, pad)
    for x in range(CX):
        lap[x] = laplacian(x, src, lo, hi, pad)


def first_kernel(cells, amps, p0, pm, lap, c, q, p1, plo, phi, u, ulo, uhi):
    for x in range(CX):
        wsq = c[x] * c[x]
        p1[x] = 2.0 * p0[x] - pm[x] + wsq * lap[x]
        u[x] = wsq * q[x]
    ulo[...] = u[0:R]
    uhi[...] = u[CX - R :]
    add_source(p1, cells, amps[0], (plo, phi))


def forward_kernel(step, cells, amps, src, lo, hi, old, c, lap, new, nlo, nhi, pad):
    fill_pad(src, pad)
    base = pl.multiple_of(pl.program_id(0) * TY, TY)
    for x in range(CX):
        curve = laplacian(x, src, lo, hi, pad)
        lap[x] = curve
        here = src[x, pl.ds(base, TY), :]
        new[x] = 2.0 * here - old[x] + c[x] * c[x] * curve
    add_source(new, cells, amps[step], (nlo, nhi))


def last_forward_kernel(step, cells, amps, src, lo, hi, old, c, q4, img, new, grad, pad):
    fill_pad(src, pad)
    base = pl.multiple_of(pl.program_id(0) * TY, TY)
    for x in range(CX):
        curve = laplacian(x, src, lo, hi, pad)
        here = src[x, pl.ds(base, TY), :]
        new[x] = 2.0 * here - old[x] + c[x] * c[x] * curve
        grad[x] = 2.0 * c[x] * (img[x] + q4[x] * curve)
    add_source(new, cells, amps[step], None)


def residual_term(step, x, res):
    lane = lax.broadcasted_iota(jnp.int32, (TY, AZ), 1)
    at = step * CX + x
    rows = res[...]
    if at:
        rows = pltpu.roll(rows, AZ - at, 1)
    return jnp.where(lane == 0, rows, 0.0)


def adjoint_kernel(step, src, lo, hi, now, old, c, res, new, u, ulo, uhi, pad):
    fill_pad(src, pad)
    for x in range(CX):
        value = 2.0 * now[x] - old[x] + laplacian(x, src, lo, hi, pad)
        value = value + residual_term(step, x, res)
        new[x] = value
        u[x] = c[x] * c[x] * value
    ulo[...] = u[0:R]
    uhi[...] = u[CX - R :]


def image_kernel(
    step, src, lo, hi, now, old, c, res, q3, lap2, lap1, lap0, new, u, ulo, uhi, img, pad
):
    adjoint_kernel(step, src, lo, hi, now, old, c, res, new, u, ulo, uhi, pad)
    for x in range(CX):
        img[x] = q3[x] * lap2[x] + now[x] * lap1[x] + new[x] * lap0[x]


def last_adjoint_kernel(step, src, lo, hi, now, old, res, new, pad):
    fill_pad(src, pad)
    for x in range(CX):
        value = 2.0 * now[x] - old[x] + laplacian(x, src, lo, hi, pad)
        new[x] = value + residual_term(step, x, res)


PAD_SCRATCH = pltpu.VMEM((CX, AY + 2 * PAD, AZ), F32)
RES = pl.BlockSpec((TY, AZ), lambda i, *_: (i, 0))


def run(kernel, scalars, args, in_specs, outs, stencil=True, flops=10_000_000):
    shapes = {"s": (SLAB, BLOCK), "h": (HALO, HBLOCK)}
    kinds = [shapes[k] for k in outs]
    traffic = sum(a.size * 4 for a in args) + sum(4 * s[0] * s[1] * s[2] for s, _ in kinds)
    return pl.pallas_call(
        kernel,
        grid_spec=pltpu.PrefetchScalarGridSpec(
            num_scalar_prefetch=len(scalars),
            grid=(KY,),
            in_specs=in_specs,
            out_specs=[b for _, b in kinds],
            scratch_shapes=[PAD_SCRATCH] if stencil else [],
        ),
        out_shape=[sds(s) for s, _ in kinds],
        compiler_params=pltpu.CompilerParams(vmem_limit_bytes=VMEM),
        cost_estimate=pl.CostEstimate(flops=flops, bytes_accessed=traffic, transcendentals=0),
    )(*scalars, *args)


STENCIL = [WHOLE, HBLOCK, HBLOCK]


def pick_kernel(which, slot, b0, b1, b2, b3, out, sem):
    bufs = (b0, b1, b2, b3)
    for i in range(KY):
        for b in range(N_SHOT):

            @pl.when(which[i] == b)
            def _():
                pltpu.make_async_copy(
                    bufs[b].at[slot[i]], out.at[:, pl.ds(i * TY, TY), :], sem.at[i]
                ).start()

    for i in range(KY):
        pltpu.make_async_copy(
            b0.at[slot[i]], out.at[:, pl.ds(i * TY, TY), :], sem.at[i]
        ).wait()


def pick_tiles(which, slot, bufs):
    return pl.pallas_call(
        pick_kernel,
        grid_spec=pltpu.PrefetchScalarGridSpec(
            num_scalar_prefetch=2,
            grid=(1,),
            in_specs=[pl.BlockSpec(memory_space=pl.ANY)] * 4,
            out_specs=pl.BlockSpec(memory_space=pl.ANY),
            scratch_shapes=[pltpu.SemaphoreType.DMA((KY,))],
        ),
        out_shape=sds(SLAB),
    )(which, slot, *bufs)


def pack_kernel(tile_of, slab, o0, o1, o2, o3, sem):
    outs = (o0, o1, o2, o3)
    copies = []
    for b in range(N_SHOT):
        for k in range(SHARE):
            n = b * SHARE + k
            start = pl.multiple_of(tile_of[n] * TY, TY)
            copies.append(
                pltpu.make_async_copy(slab.at[:, pl.ds(start, TY), :], outs[b].at[k], sem.at[n])
            )
    for copy in copies:
        copy.start()
    for copy in copies:
        copy.wait()


def pack_tiles(tile_of, slab):
    part = sds((SHARE, CX, TY, AZ))
    return pl.pallas_call(
        pack_kernel,
        grid_spec=pltpu.PrefetchScalarGridSpec(
            num_scalar_prefetch=1,
            grid=(1,),
            in_specs=[pl.BlockSpec(memory_space=pl.ANY)],
            out_specs=[pl.BlockSpec(memory_space=pl.ANY)] * 4,
            scratch_shapes=[pltpu.SemaphoreType.DMA((N_SHOT * SHARE,))],
        ),
        out_shape=[part] * 4,
    )(tile_of, slab)


def merge_kernel(used, b0, b1, b2, b3, out):
    slot = pl.program_id(0)
    bufs = (b0, b1, b2, b3)
    for half in range(2):
        total = jnp.zeros((CX, TY, AZ), F32)
        for b in range(N_SHOT):
            total = total + jnp.where(used[(b * SHARE + slot) * 2 + half] == 1, bufs[b][0], 0.0)
        out[half, 0] = total


def merge_tiles(used, bufs):
    spec = pl.BlockSpec((1, CX, TY, AZ), lambda k, *_: (k, 0, 0, 0))
    return pl.pallas_call(
        merge_kernel,
        grid_spec=pltpu.PrefetchScalarGridSpec(
            num_scalar_prefetch=1,
            grid=(SHARE,),
            in_specs=[spec] * 4,
            out_specs=pl.BlockSpec((2, 1, CX, TY, AZ), lambda k, *_: (0, k, 0, 0, 0)),
        ),
        out_shape=sds((2, SHARE, CX, TY, AZ)),
        compiler_params=pltpu.CompilerParams(vmem_limit_bytes=VMEM),
    )(used, *bufs)


def within_shots(value, flip):
    return lax.ppermute(value, "shot", [(s, s ^ flip) for s in range(N_SHOT)])


def shift_shot(value, shot, steps):
    pairs = []
    for s in range(N_SHOT):
        for j in range(N_SUB):
            to = (j + steps) % N_SUB if s == shot else j
            pairs.append((s * N_SUB + j, s * N_SUB + to))
    return lax.ppermute(value, ("shot", "sub"), pairs)


def shift_all(value, amounts, sign):
    for shot in range(N_SHOT):
        branches = [lambda v: v]
        for k in range(1, N_SUB):
            branches.append(functools.partial(shift_shot, shot=shot, steps=sign * k))
        value = lax.switch(amounts[shot], branches, value)
    return value


def exchange(low_planes, high_planes, my_sub):
    up = [(i, i + 1) for i in range(N_SUB - 1)]
    down = [(b, a) for a, b in up]
    before = lax.ppermute(high_planes, "sub", up)
    after = lax.ppermute(low_planes, "sub", down)
    return before, after


def body(
    courant_tiles,
    tile_place,
    anchors,
    source_cells,
    wavelet,
    forward_state,
    adjoint_state,
    residual,
):
    my_shot = lax.axis_index("shot")
    my_sub = lax.axis_index("sub")
    start_x = anchors[:, 0]
    start_y = anchors[:, 1]
    amounts = start_x % N_SUB
    upper = (my_sub < start_x).astype(jnp.int32)
    column = my_sub + upper * N_SUB
    ids = start_y[:, None] + jnp.arange(KY, dtype=jnp.int32)[None, :]
    places = tile_place[column[:, None], ids]
    own_places = places[my_shot]

    pm, p0 = forward_state[0, 0], forward_state[0, 1]
    q5, q4 = adjoint_state[0, 0], adjoint_state[0, 1]

    bufs = []
    for flip in range(N_SHOT):
        mine = lax.dynamic_slice_in_dim(courant_tiles, upper[my_shot ^ flip] * SHARE, SHARE, 0)
        bufs.append(within_shots(mine, flip) if flip else mine)
    which = (own_places // SHARE) ^ my_shot
    slot = own_places % SHARE
    before, after = exchange(p0[0:R], p0[CX - R :], my_sub)
    slab = pick_tiles(which, slot, bufs)
    (lap0,) = run(lap_kernel, (), (p0, before, after), STENCIL, "s")
    c = shift_all(slab, amounts, -1)

    cells = source_cells[my_shot] - jnp.stack([my_sub * CX, 0, 0]).astype(jnp.int32)
    amps = wavelet[0]
    res = jnp.pad(
        residual[0].reshape(STEPS * CX, AY).T, ((0, 0), (0, AZ - STEPS * CX))
    )

    p1, plo, phi, u, ulo, uhi = run(
        first_kernel, (cells, amps), (p0, pm, lap0, c, q4), [BLOCK] * 5, "shhshh", stencil=False
    )
    ub, ua = exchange(ulo, uhi, my_sub)
    pb, pa = exchange(plo, phi, my_sub)
    q3, u, ulo, uhi = run(
        functools.partial(adjoint_kernel, 0),
        (),
        (u, ub, ua, q4, q5, c, res),
        STENCIL + [BLOCK] * 3 + [RES],
        "sshh",
    )
    ub, ua = exchange(ulo, uhi, my_sub)
    lap1, p2, plo, phi = run(
        functools.partial(forward_kernel, 1),
        (cells, amps),
        (p1, pb, pa, p0, c),
        STENCIL + [BLOCK] * 2,
        "sshh",
    )
    pb, pa = exchange(plo, phi, my_sub)
    q2, u, ulo, uhi = run(
        functools.partial(adjoint_kernel, 1),
        (),
        (u, ub, ua, q3, q4, c, res),
        STENCIL + [BLOCK] * 3 + [RES],
        "sshh",
    )
    ub, ua = exchange(ulo, uhi, my_sub)
    lap2, p3, plo, phi = run(
        functools.partial(forward_kernel, 2),
        (cells, amps),
        (p2, pb, pa, p1, c),
        STENCIL + [BLOCK] * 2,
        "sshh",
    )
    pb, pa = exchange(plo, phi, my_sub)
    q1, u, ulo, uhi, img = run(
        functools.partial(image_kernel, 2),
        (),
        (u, ub, ua, q2, q3, c, res, q3, lap2, lap1, lap0),
        STENCIL + [BLOCK] * 3 + [RES] + [BLOCK] * 4,
        "sshhs",
    )
    ub, ua = exchange(ulo, uhi, my_sub)
    p4, grad = run(
        functools.partial(last_forward_kernel, 3),
        (cells, amps),
        (p3, pb, pa, p2, c, q4, img),
        STENCIL + [BLOCK] * 4,
        "ss",
    )
    (q0,) = run(
        functools.partial(last_adjoint_kernel, 3),
        (),
        (u, ub, ua, q1, q2, res),
        STENCIL + [BLOCK] * 2 + [RES],
        "s",
    )

    back = shift_all(grad, amounts, 1)
    holder = jnp.arange(N_SHOT, dtype=jnp.int32)[:, None] ^ my_shot
    spot = holder * SHARE + jnp.arange(SHARE, dtype=jnp.int32)[None, :]
    match = spot.reshape(-1)[:, None] == own_places[None, :]
    tile_of = jnp.sum(
        jnp.where(match, jnp.arange(KY, dtype=jnp.int32)[None, :], 0), axis=1, dtype=jnp.int32
    )
    parts = pack_tiles(tile_of, back)
    got = [within_shots(part, flip) if flip else part for flip, part in enumerate(parts)]
    source = jnp.arange(N_SHOT, dtype=jnp.int32) ^ my_shot
    mine = my_shot * SHARE + jnp.arange(SHARE, dtype=jnp.int32)
    covered = jnp.any(places[source][:, None, :] == mine[None, :, None], axis=2)
    side = upper[source][:, None, None] == jnp.arange(2, dtype=jnp.int32)[None, None, :]
    used = (covered[:, :, None] & side).astype(jnp.int32).reshape(-1)
    gradient_tiles = merge_tiles(used, got).reshape(courant_tiles.shape)

    return (jnp.stack([p3, p4])[None], jnp.stack([q1, q0])[None], gradient_tiles)


def solution(mesh):
    return jax.shard_map(
        body,
        mesh=mesh,
        in_specs=(
            P(("shot", "sub"), None, None, None),
            P(),
            P(),
            P(),
            P("shot", None),
            P("shot", None, "sub", None, None),
            P("shot", None, "sub", None, None),
            P("shot", None, "sub", None),
        ),
        out_specs=(
            P("shot", None, "sub", None, None),
            P("shot", None, "sub", None, None),
            P(("shot", "sub"), None, None, None),
        ),
        check_vma=False,
    )
```

```python
import functools

import jax
import jax.numpy as jnp
from jax import lax
from jax.experimental import pallas as pl
from jax.experimental.pallas import tpu as pltpu
from jax.sharding import PartitionSpec as P

CX = 6
TY = 64
AZ = 128
KY = 6
AY = KY * TY
STEPS = 4
N_SHOT = 4
N_SUB = 32
SHARE = 3
R = 4
PAD = 8

WEIGHTS = (1.6, -0.2, 8.0 / 315.0, -1.0 / 560.0)
CENTER = -205.0 / 72.0 * 3.0

F32 = jnp.float32
HY = TY // 2
CHUNK = (CX, KY * HY, AZ)
CHALO = (R, KY * HY, AZ)
SLAB = (CX, AY, AZ)
HALO = (R, AY, AZ)
PAIR = (2, CX, AY, AZ)
BLOCK = pl.BlockSpec((CX, TY, AZ), lambda i, *_: (0, i, 0))
HBLOCK = pl.BlockSpec((R, TY, AZ), lambda i, *_: (0, i, 0))
WHOLE = pl.BlockSpec(SLAB, lambda i, *_: (0, 0, 0))
CBLOCK = pl.BlockSpec((CX, HY, AZ), lambda i, *_: (0, i, 0))
CHBLOCK = pl.BlockSpec((R, HY, AZ), lambda i, *_: (0, i, 0))
CWHOLE = pl.BlockSpec(CHUNK, lambda i, *_: (0, 0, 0))
PAIR0 = pl.BlockSpec((1, CX, TY, AZ), lambda i, *_: (0, 0, i, 0))
PAIR1 = pl.BlockSpec((1, CX, TY, AZ), lambda i, *_: (1, 0, i, 0))
PAIR0_WHOLE = pl.BlockSpec((1, CX, AY, AZ), lambda i, *_: (0, 0, 0, 0))
RES = pl.BlockSpec((TY, AZ), lambda i, *_: (i, 0))
VMEM = 20 * 1024 * 1024


def half_block(h):
    return pl.BlockSpec((CX, HY, AZ), lambda i, *_: (0, 2 * i + h, 0))


def half_pair1(h):
    return pl.BlockSpec((1, CX, HY, AZ), lambda i, *_: (1, 0, 2 * i + h, 0))


def sds(shape):
    return jax.ShapeDtypeStruct(shape, F32)


def rows(refs, x):
    if len(refs) == 1:
        return refs[0][x]
    return jnp.concatenate([refs[0][x], refs[1][x]], axis=0)


def fill_pad(src, pad):
    @pl.when(pl.program_id(0) == 0)
    def _():
        pad[:, 0:PAD, :] = jnp.zeros((CX, PAD, AZ), F32)
        pad[:, PAD + AY :, :] = jnp.zeros((CX, PAD, AZ), F32)
        if len(src) == 1:
            pad[:, PAD : PAD + AY, :] = src[0][...]
        else:
            for i in range(KY):
                for h in range(2):
                    at = PAD + i * TY + h * HY
                    pad[:, at : at + HY, :] = src[h][:, i * HY : (i + 1) * HY, :]


def centre(x, base, size, pad):
    return pad[x, pl.ds(base + PAD, size), :]


def laplacian(x, base, size, pad, lo, hi):
    def plane(k):
        if k < 0:
            return rows(lo, k + R)
        if k >= CX:
            return rows(hi, k - CX)
        return centre(k, base, size, pad)

    here = plane(x)
    lane = lax.broadcasted_iota(jnp.int32, (size, AZ), 1)
    out = CENTER * here
    for r, w in enumerate(WEIGHTS, 1):
        out = out + w * (plane(x + r) + plane(x - r))
    for r, w in enumerate(WEIGHTS, 1):
        out = out + w * (
            pad[x, pl.ds(base + (PAD + r), size), :] + pad[x, pl.ds(base + (PAD - r), size), :]
        )
    for r, w in enumerate(WEIGHTS, 1):
        up = jnp.where(lane < AZ - r, pltpu.roll(here, AZ - r, 1), 0.0)
        down = jnp.where(lane >= r, pltpu.roll(here, r, 1), 0.0)
        out = out + w * (up + down)
    return out


def add_source(out, cells, amp, base, size):
    col = cells[1] - base
    inside = (cells[0] >= 0) & (cells[0] < CX) & (col >= 0) & (col < size)

    @pl.when(inside)
    def _():
        lane = lax.broadcasted_iota(jnp.int32, (1, 1, AZ), 2)
        x = cells[0]
        row = out[pl.ds(x, 1), pl.ds(col, 1), :]
        out[pl.ds(x, 1), pl.ds(col, 1), :] = row + jnp.where(lane == cells[2], amp, 0.0)


def send_planes(value, lo, hi):
    for k in range(R):
        low, high = value[k], value[CX - R + k]
        if len(lo) == 1:
            lo[0][k] = low
            hi[0][k] = high
        else:
            lo[0][k], lo[1][k] = low[:HY], low[HY:]
            hi[0][k], hi[1][k] = high[:HY], high[HY:]


def block_base(h=None):
    base = pl.multiple_of(pl.program_id(0) * TY, TY)
    return base if h is None else base + h * HY


def lap_kernel(src, lo, hi, lap, pad):
    fill_pad([src], pad)
    for x in range(CX):
        lap[x] = laplacian(x, block_base(), TY, pad, [lo], [hi])


def first_kernel(h, cells, amps, p0, pm, lap, q, c, p1, plo, phi, u, ulo, uhi):
    for x in range(CX):
        wsq = c[x] * c[x]
        p1[x] = 2.0 * p0[x] - pm[x] + wsq * lap[x]
        u[x] = wsq * q[x]
    add_source(p1, cells, amps[0], block_base(h), HY)
    send_planes(u, [ulo], [uhi])
    send_planes(p1, [plo], [phi])


def residual_term(step, x, res):
    lane = lax.broadcasted_iota(jnp.int32, (TY, AZ), 1)
    at = step * CX + x
    values = res[...]
    if at:
        values = pltpu.roll(values, AZ - at, 1)
    return jnp.where(lane == 0, values, 0.0)


def adjoint_first_kernel(
    s0, s1, lo0, lo1, hi0, hi1, now, old, c0, c1, res, new, u, ulo, uhi, pad
):
    fill_pad([s0, s1], pad)
    for x in range(CX):
        curve = laplacian(x, block_base(), TY, pad, [lo0, lo1], [hi0, hi1])
        value = 2.0 * now[x] - old[x] + curve + residual_term(0, x, res)
        wave = rows([c0, c1], x)
        new[x] = value
        u[x] = wave * wave * value
    send_planes(u, [ulo], [uhi])


def adjoint_kernel(step, src, lo, hi, now, old, c0, c1, res, new, u, ulo, uhi, pad):
    fill_pad([src], pad)
    for x in range(CX):
        curve = laplacian(x, block_base(), TY, pad, [lo], [hi])
        value = 2.0 * now[x] - old[x] + curve + residual_term(step, x, res)
        wave = rows([c0, c1], x)
        new[x] = value
        u[x] = wave * wave * value
    send_planes(u, [ulo], [uhi])


def image_kernel(
    src, lo, hi, now, old, c0, c1, res, lap2, lap1, lap0, pair, u, ulo, uhi, img, pad
):
    new = pair.at[0]
    adjoint_kernel(2, src, lo, hi, now, old, c0, c1, res, new, u, ulo, uhi, pad)
    for x in range(CX):
        img[x] = old[x] * lap2[x] + now[x] * lap1[x] + new[x] * lap0[x]


def last_adjoint_kernel(src, lo, hi, now, old, res, pair, pad):
    fill_pad([src], pad)
    for x in range(CX):
        curve = laplacian(x, block_base(), TY, pad, [lo], [hi])
        pair[0, x] = 2.0 * now[0, x] - old[x] + curve + residual_term(3, x, res)


def forward_second_kernel(
    cells, amps, s0, s1, lo0, lo1, hi0, hi1, old, c0, c1, lap, new, nlo, nhi, pad
):
    fill_pad([s0, s1], pad)
    base = block_base()
    for x in range(CX):
        curve = laplacian(x, base, TY, pad, [lo0, lo1], [hi0, hi1])
        wave = rows([c0, c1], x)
        lap[x] = curve
        new[x] = 2.0 * centre(x, base, TY, pad) - old[x] + wave * wave * curve
    add_source(new, cells, amps[1], base, TY)
    send_planes(new, [nlo], [nhi])


def forward_third_kernel(
    cells, amps, src, lo, hi, old0, old1, c0, c1, lap, pair, nlo0, nlo1, nhi0, nhi1, pad
):
    new = pair.at[0]
    fill_pad([src], pad)
    base = block_base()
    for x in range(CX):
        curve = laplacian(x, base, TY, pad, [lo], [hi])
        wave = rows([c0, c1], x)
        lap[x] = curve
        new[x] = 2.0 * centre(x, base, TY, pad) - rows([old0, old1], x) + wave * wave * curve
    add_source(new, cells, amps[2], base, TY)
    send_planes(new, [nlo0, nlo1], [nhi0, nhi1])


def last_forward_kernel(h, cells, amps, src, lo, hi, old, c, q4, img, pair, grad, pad):
    fill_pad([src.at[0]], pad)
    new = pair.at[0]
    base = block_base(h)
    for x in range(CX):
        curve = laplacian(x, base, HY, pad, [lo], [hi])
        wave = c[x]
        new[x] = 2.0 * centre(x, base, HY, pad) - old[x] + wave * wave * curve
        grad[x] = 2.0 * wave * (img[x] + q4[x] * curve)
    add_source(new, cells, amps[3], base, HY)


PAD_SCRATCH = pltpu.VMEM((CX, AY + 2 * PAD, AZ), F32)
OUTS = {
    "s": (SLAB, BLOCK),
    "h": (HALO, HBLOCK),
    "c": (CHUNK, CBLOCK),
    "d": (CHALO, CHBLOCK),
    "0": (PAIR, PAIR0),
    "1": (PAIR, PAIR1),
    "p": (PAIR, half_pair1(0)),
    "q": (PAIR, half_pair1(1)),
}


def size_of(shape):
    total = 4
    for n in shape:
        total *= n
    return total


def run(kernel, scalars, args, in_specs, outs, stencil=True, flops=10_000_000, aliases=None):
    kinds = [OUTS[k] for k in outs]
    traffic = sum(size_of(a.shape) for a in args) + sum(size_of(s) for s, _ in kinds)
    return pl.pallas_call(
        kernel,
        grid_spec=pltpu.PrefetchScalarGridSpec(
            num_scalar_prefetch=len(scalars),
            grid=(KY,),
            in_specs=in_specs,
            out_specs=[b for _, b in kinds],
            scratch_shapes=[PAD_SCRATCH] if stencil else [],
        ),
        out_shape=[sds(s) for s, _ in kinds],
        input_output_aliases=aliases or {},
        compiler_params=pltpu.CompilerParams(vmem_limit_bytes=VMEM),
        cost_estimate=pl.CostEstimate(flops=flops, bytes_accessed=traffic, transcendentals=0),
    )(*scalars, *args)


STENCIL = [WHOLE, HBLOCK, HBLOCK]
HALVES = [CWHOLE] * 2 + [CHBLOCK] * 4


def pick_kernel(which, slot, b0, b1, b2, b3, out):
    for b, ref in enumerate((b0, b1, b2, b3)):

        @pl.when(which[pl.program_id(0)] == b)
        def _():
            out[...] = ref[0]


def pick_tiles(which, slot, bufs):
    spec = pl.BlockSpec((1, CX, HY, AZ), lambda i, which, slot: (slot[i], 0, 0, 0))
    return pl.pallas_call(
        pick_kernel,
        grid_spec=pltpu.PrefetchScalarGridSpec(
            num_scalar_prefetch=2,
            grid=(KY,),
            in_specs=[spec] * 4,
            out_specs=CBLOCK,
        ),
        out_shape=sds(CHUNK),
    )(which, slot, *bufs)


def pack_kernel(tile_of, s0, s1, s2, s3, o0, o1, o2, o3):
    for src, out in ((s0, o0), (s1, o1), (s2, o2), (s3, o3)):
        out[0] = src[...]


def pack_tiles(tile_of, slab):
    part = sds((SHARE, CX, HY, AZ))

    def at(b):
        return pl.BlockSpec((CX, HY, AZ), lambda k, tile_of: (0, tile_of[b * SHARE + k], 0))

    return pl.pallas_call(
        pack_kernel,
        grid_spec=pltpu.PrefetchScalarGridSpec(
            num_scalar_prefetch=1,
            grid=(SHARE,),
            in_specs=[at(b) for b in range(N_SHOT)],
            out_specs=[pl.BlockSpec((1, CX, HY, AZ), lambda k, tile_of: (k, 0, 0, 0))] * 4,
        ),
        out_shape=[part] * 4,
    )(tile_of, *[slab] * 4)


def merge_kernel(used, *refs):
    out = refs[-1]
    slot = pl.program_id(0)
    for side in range(2):
        for h in range(2):
            total = jnp.zeros((CX, HY, AZ), F32)
            for b in range(N_SHOT):
                part = refs[h * N_SHOT + b][0]
                total = total + jnp.where(used[(b * SHARE + slot) * 2 + side] == 1, part, 0.0)
            out[side, 0, :, h * HY : (h + 1) * HY, :] = total


def merge_tiles(used, bufs):
    spec = pl.BlockSpec((1, CX, HY, AZ), lambda k, *_: (k, 0, 0, 0))
    return pl.pallas_call(
        merge_kernel,
        grid_spec=pltpu.PrefetchScalarGridSpec(
            num_scalar_prefetch=1,
            grid=(SHARE,),
            in_specs=[spec] * len(bufs),
            out_specs=pl.BlockSpec((2, 1, CX, TY, AZ), lambda k, *_: (0, k, 0, 0, 0)),
        ),
        out_shape=sds((2, SHARE, CX, TY, AZ)),
        compiler_params=pltpu.CompilerParams(vmem_limit_bytes=VMEM),
    )(used, *bufs)


def within_shots(value, flip):
    return lax.ppermute(value, "shot", [(s, s ^ flip) for s in range(N_SHOT)])


def shift_column(value, amount, sign):
    def moved(value, steps):
        return lax.ppermute(value, "sub", [(j, (j + steps) % N_SUB) for j in range(N_SUB)])

    branches = [lambda v: v]
    for k in range(1, N_SUB):
        branches.append(functools.partial(moved, steps=sign * k))
    return lax.switch(amount, branches, value)


def exchange(low_planes, high_planes):
    up = [(i, i + 1) for i in range(N_SUB - 1)]
    down = [(b, a) for a, b in up]
    before = lax.ppermute(high_planes, "sub", up)
    after = lax.ppermute(low_planes, "sub", down)
    return before, after


def body(
    courant_tiles,
    tile_place,
    anchors,
    source_cells,
    wavelet,
    forward_state,
    adjoint_state,
    residual,
):
    my_shot = lax.axis_index("shot")
    my_sub = lax.axis_index("sub")
    start_x = anchors[:, 0]
    start_y = anchors[:, 1]
    amounts = start_x % N_SUB
    upper = (my_sub < start_x).astype(jnp.int32)
    column = my_sub + upper * N_SUB
    ids = start_y[:, None] + jnp.arange(KY, dtype=jnp.int32)[None, :]
    places = tile_place[column[:, None], ids]
    own_places = places[my_shot]

    pm, p0 = forward_state[0, 0], forward_state[0, 1]
    q5, q4 = adjoint_state[0, 0], adjoint_state[0, 1]

    bufs = []
    for h in range(2):
        half = lax.slice_in_dim(courant_tiles, h * HY, (h + 1) * HY, axis=2)
        parts = []
        for flip in range(N_SHOT):
            mine = lax.dynamic_slice_in_dim(half, upper[my_shot ^ flip] * SHARE, SHARE, 0)
            parts.append(within_shots(mine, flip) if flip else mine)
        bufs.append(parts)
    which = (own_places // SHARE) ^ my_shot
    slot = own_places % SHARE
    amount = amounts[my_shot]
    before, after = exchange(p0[0:R], p0[CX - R :])
    (lap0,) = run(lap_kernel, (), (p0, before, after), STENCIL, "s")

    cells = source_cells[my_shot] - jnp.stack([my_sub * CX, 0, 0]).astype(jnp.int32)
    amps = wavelet[0]
    source = (cells, amps)
    res = jnp.pad(
        residual[0].reshape(STEPS * CX, AY).T, ((0, 0), (0, AZ - STEPS * CX))
    )

    c, p1, u4, ub, ua, pb, pa = [], [], [], [], [], [], []
    for h in range(2):
        ch = shift_column(pick_tiles(which, slot, bufs[h]), amount, -1)
        p, plo, phi, u, ulo, uhi = run(
            functools.partial(first_kernel, h),
            source,
            (p0, pm, lap0, q4, ch),
            [half_block(h)] * 4 + [CBLOCK],
            "cddcdd",
            stencil=False,
        )
        c.append(ch)
        p1.append(p)
        u4.append(u)
        b, a = exchange(ulo, uhi)
        ub.append(b)
        ua.append(a)
        b, a = exchange(plo, phi)
        pb.append(b)
        pa.append(a)

    q3, u, ulo, uhi = run(
        adjoint_first_kernel,
        (),
        (*u4, *ub, *ua, q4, q5, *c, res),
        HALVES + [BLOCK] * 2 + [CBLOCK] * 2 + [RES],
        "sshh",
    )
    ub, ua = exchange(ulo, uhi)
    lap1, p2, plo, phi = run(
        forward_second_kernel,
        source,
        (*p1, *pb, *pa, p0, *c),
        HALVES + [BLOCK] + [CBLOCK] * 2,
        "sshh",
    )
    pb, pa = exchange(plo, phi)
    q2, u, ulo, uhi = run(
        functools.partial(adjoint_kernel, 1),
        (),
        (u, ub, ua, q3, q4, *c, res),
        STENCIL + [BLOCK] * 2 + [CBLOCK] * 2 + [RES],
        "sshh",
    )
    ub, ua = exchange(ulo, uhi)
    lap2, forward_out, plo0, plo1, phi0, phi1 = run(
        forward_third_kernel,
        source,
        (p2, pb, pa, *p1, *c),
        STENCIL + [CBLOCK] * 4,
        "s0dddd",
    )
    planes = [exchange(plo0, phi0), exchange(plo1, phi1)]
    adjoint_out, u, ulo, uhi, img = run(
        image_kernel,
        (),
        (u, ub, ua, q2, q3, *c, res, lap2, lap1, lap0),
        STENCIL + [BLOCK] * 2 + [CBLOCK] * 2 + [RES] + [BLOCK] * 3,
        "0shhs",
    )
    ub, ua = exchange(ulo, uhi)

    holder = jnp.arange(N_SHOT, dtype=jnp.int32)[:, None] ^ my_shot
    spot = holder * SHARE + jnp.arange(SHARE, dtype=jnp.int32)[None, :]
    match = spot.reshape(-1)[:, None] == own_places[None, :]
    tile_of = jnp.sum(
        jnp.where(match, jnp.arange(KY, dtype=jnp.int32)[None, :], 0), axis=1, dtype=jnp.int32
    )
    got = []
    for h in range(2):
        forward_out, grad = run(
            functools.partial(last_forward_kernel, h),
            source,
            (forward_out, *planes[h], p2, c[h], q4, img),
            [PAIR0_WHOLE, CHBLOCK, CHBLOCK, half_block(h), CBLOCK] + [half_block(h)] * 2,
            "pq"[h] + "c",
            aliases={2: 0},
        )
        parts = pack_tiles(tile_of, shift_column(grad, amount, 1))
        got += [within_shots(part, flip) if flip else part for flip, part in enumerate(parts)]
    (adjoint_out,) = run(
        last_adjoint_kernel,
        (),
        (u, ub, ua, adjoint_out, q2, res),
        STENCIL + [PAIR0, BLOCK, RES],
        "1",
        aliases={3: 0},
    )
    shots = jnp.arange(N_SHOT, dtype=jnp.int32) ^ my_shot
    mine = my_shot * SHARE + jnp.arange(SHARE, dtype=jnp.int32)
    covered = jnp.any(places[shots][:, None, :] == mine[None, :, None], axis=2)
    side = upper[shots][:, None, None] == jnp.arange(2, dtype=jnp.int32)[None, None, :]
    used = (covered[:, :, None] & side).astype(jnp.int32).reshape(-1)
    gradient_tiles = merge_tiles(used, got).reshape(courant_tiles.shape)

    return forward_out[None], adjoint_out[None], gradient_tiles


def solution(mesh):
    return jax.shard_map(
        body,
        mesh=mesh,
        in_specs=(
            P(("shot", "sub"), None, None, None),
            P(),
            P(),
            P(),
            P("shot", None),
            P("shot", None, "sub", None, None),
            P("shot", None, "sub", None, None),
            P("shot", None, "sub", None),
        ),
        out_specs=(
            P("shot", None, "sub", None, None),
            P("shot", None, "sub", None, None),
            P(("shot", "sub"), None, None, None),
        ),
        check_vma=False,
    )
```

```python
import functools

import jax
import jax.numpy as jnp
from jax import lax
from jax.experimental import pallas as pl
from jax.experimental.pallas import tpu as pltpu
from jax.sharding import PartitionSpec as P

CX = 6
TY = 64
AZ = 128
KY = 6
AY = KY * TY
STEPS = 4
N_SHOT = 4
N_SUB = 32
SHARE = 3
R = 4
PAD = 8

WEIGHTS = (1.6, -0.2, 8.0 / 315.0, -1.0 / 560.0)
CENTER = -205.0 / 72.0 * 3.0

F32 = jnp.float32
SLAB = (CX, AY, AZ)
HALO = (R, AY, AZ)
PAIR = (2, CX, AY, AZ)
BLOCK = pl.BlockSpec((CX, TY, AZ), lambda i, *_: (0, i, 0))
HBLOCK = pl.BlockSpec((R, TY, AZ), lambda i, *_: (0, i, 0))
WHOLE = pl.BlockSpec(SLAB, lambda i, *_: (0, 0, 0))
PAIR0 = pl.BlockSpec((1, CX, TY, AZ), lambda i, *_: (0, 0, i, 0))
PAIR1 = pl.BlockSpec((1, CX, TY, AZ), lambda i, *_: (1, 0, i, 0))
PAIR0_WHOLE = pl.BlockSpec((1, CX, AY, AZ), lambda i, *_: (0, 0, 0, 0))
RES = pl.BlockSpec((TY, AZ), lambda i, *_: (i, 0))
VMEM = 20 * 1024 * 1024


def sds(shape):
    return jax.ShapeDtypeStruct(shape, F32)


def fill_pad(src, pad):
    @pl.when(pl.program_id(0) == 0)
    def _():
        pad[:, 0:PAD, :] = jnp.zeros((CX, PAD, AZ), F32)
        pad[:, PAD + AY :, :] = jnp.zeros((CX, PAD, AZ), F32)
        pad[:, PAD : PAD + AY, :] = src[...]


def centre(x, base, pad):
    return pad[x, pl.ds(base + PAD, TY), :]


def laplacian(x, base, pad, lo, hi):
    def plane(k):
        if k < 0:
            return lo[k + R]
        if k >= CX:
            return hi[k - CX]
        return centre(k, base, pad)

    here = plane(x)
    lane = lax.broadcasted_iota(jnp.int32, (TY, AZ), 1)
    out = CENTER * here
    for r, w in enumerate(WEIGHTS, 1):
        out = out + w * (plane(x + r) + plane(x - r))
    for r, w in enumerate(WEIGHTS, 1):
        out = out + w * (
            pad[x, pl.ds(base + (PAD + r), TY), :] + pad[x, pl.ds(base + (PAD - r), TY), :]
        )
    for r, w in enumerate(WEIGHTS, 1):
        up = jnp.where(lane < AZ - r, pltpu.roll(here, AZ - r, 1), 0.0)
        down = jnp.where(lane >= r, pltpu.roll(here, r, 1), 0.0)
        out = out + w * (up + down)
    return out


def add_source(out, cells, amp, base):
    col = cells[1] - base
    inside = (cells[0] >= 0) & (cells[0] < CX) & (col >= 0) & (col < TY)

    @pl.when(inside)
    def _():
        lane = lax.broadcasted_iota(jnp.int32, (1, 1, AZ), 2)
        x = cells[0]
        row = out[pl.ds(x, 1), pl.ds(col, 1), :]
        out[pl.ds(x, 1), pl.ds(col, 1), :] = row + jnp.where(lane == cells[2], amp, 0.0)


def send_planes(value, lo, hi):
    lo[...] = value[0:R]
    hi[...] = value[CX - R :]


def block_base():
    return pl.multiple_of(pl.program_id(0) * TY, TY)


def lap_kernel(src, lo, hi, lap, pad):
    fill_pad(src, pad)
    for x in range(CX):
        lap[x] = laplacian(x, block_base(), pad, lo, hi)


def first_kernel(cells, amps, p0, pm, lap, q, c, p1, plo, phi, u, ulo, uhi):
    for x in range(CX):
        wsq = c[x] * c[x]
        p1[x] = 2.0 * p0[x] - pm[x] + wsq * lap[x]
        u[x] = wsq * q[x]
    add_source(p1, cells, amps[0], block_base())
    send_planes(u, ulo, uhi)
    send_planes(p1, plo, phi)


def residual_term(step, x, res):
    lane = lax.broadcasted_iota(jnp.int32, (TY, AZ), 1)
    at = step * CX + x
    values = res[...]
    if at:
        values = pltpu.roll(values, AZ - at, 1)
    return jnp.where(lane == 0, values, 0.0)


def adjoint_kernel(step, src, lo, hi, now, old, c, res, new, u, ulo, uhi, pad):
    fill_pad(src, pad)
    for x in range(CX):
        curve = laplacian(x, block_base(), pad, lo, hi)
        value = 2.0 * now[x] - old[x] + curve + residual_term(step, x, res)
        new[x] = value
        u[x] = c[x] * c[x] * value
    send_planes(u, ulo, uhi)


def image_kernel(src, lo, hi, now, old, c, res, lap2, lap1, lap0, pair, u, ulo, uhi, img, pad):
    new = pair.at[0]
    adjoint_kernel(2, src, lo, hi, now, old, c, res, new, u, ulo, uhi, pad)
    for x in range(CX):
        img[x] = old[x] * lap2[x] + now[x] * lap1[x] + new[x] * lap0[x]


def last_adjoint_kernel(src, lo, hi, now, old, res, pair, pad):
    fill_pad(src, pad)
    for x in range(CX):
        curve = laplacian(x, block_base(), pad, lo, hi)
        pair[0, x] = 2.0 * now[0, x] - old[x] + curve + residual_term(3, x, res)


def forward_kernel(step, cells, amps, src, lo, hi, old, c, lap, new, nlo, nhi, pad):
    fill_pad(src, pad)
    base = block_base()
    for x in range(CX):
        curve = laplacian(x, base, pad, lo, hi)
        lap[x] = curve
        new[x] = 2.0 * centre(x, base, pad) - old[x] + c[x] * c[x] * curve
    add_source(new, cells, amps[step], base)
    send_planes(new, nlo, nhi)


def third_forward_kernel(cells, amps, src, lo, hi, old, c, lap, pair, nlo, nhi, pad):
    new = pair.at[0]
    forward_kernel(2, cells, amps, src, lo, hi, old, c, lap, new, nlo, nhi, pad)


def last_forward_kernel(cells, amps, src, lo, hi, old, c, q4, img, pair, grad, pad):
    fill_pad(src.at[0], pad)
    new = pair.at[0]
    base = block_base()
    for x in range(CX):
        curve = laplacian(x, base, pad, lo, hi)
        new[x] = 2.0 * centre(x, base, pad) - old[x] + c[x] * c[x] * curve
        grad[x] = 2.0 * c[x] * (img[x] + q4[x] * curve)
    add_source(new, cells, amps[3], base)


PAD_SCRATCH = pltpu.VMEM((CX, AY + 2 * PAD, AZ), F32)
OUTS = {
    "s": (SLAB, BLOCK),
    "h": (HALO, HBLOCK),
    "0": (PAIR, PAIR0),
    "1": (PAIR, PAIR1),
}


def size_of(shape):
    total = 4
    for n in shape:
        total *= n
    return total


def run(kernel, scalars, args, in_specs, outs, stencil=True, flops=10_000_000, aliases=None):
    kinds = [OUTS[k] for k in outs]
    traffic = sum(size_of(a.shape) for a in args) + sum(size_of(s) for s, _ in kinds)
    return pl.pallas_call(
        kernel,
        grid_spec=pltpu.PrefetchScalarGridSpec(
            num_scalar_prefetch=len(scalars),
            grid=(KY,),
            in_specs=in_specs,
            out_specs=[b for _, b in kinds],
            scratch_shapes=[PAD_SCRATCH] if stencil else [],
        ),
        out_shape=[sds(s) for s, _ in kinds],
        input_output_aliases=aliases or {},
        compiler_params=pltpu.CompilerParams(vmem_limit_bytes=VMEM),
        cost_estimate=pl.CostEstimate(flops=flops, bytes_accessed=traffic, transcendentals=0),
    )(*scalars, *args)


STENCIL = [WHOLE, HBLOCK, HBLOCK]


def pick_kernel(which, slot, b0, b1, b2, b3, out):
    for b, ref in enumerate((b0, b1, b2, b3)):

        @pl.when(which[pl.program_id(0)] == b)
        def _():
            out[...] = ref[0]


def pick_tiles(which, slot, bufs):
    spec = pl.BlockSpec((1, CX, TY, AZ), lambda i, which, slot: (slot[i], 0, 0, 0))
    return pl.pallas_call(
        pick_kernel,
        grid_spec=pltpu.PrefetchScalarGridSpec(
            num_scalar_prefetch=2,
            grid=(KY,),
            in_specs=[spec] * 4,
            out_specs=BLOCK,
        ),
        out_shape=sds(SLAB),
    )(which, slot, *bufs)


def pack_kernel(tile_of, s0, s1, s2, s3, o0, o1, o2, o3):
    for src, out in ((s0, o0), (s1, o1), (s2, o2), (s3, o3)):
        out[0] = src[...]


def pack_tiles(tile_of, slab):
    part = sds((SHARE, CX, TY, AZ))

    def at(b):
        return pl.BlockSpec((CX, TY, AZ), lambda k, tile_of: (0, tile_of[b * SHARE + k], 0))

    return pl.pallas_call(
        pack_kernel,
        grid_spec=pltpu.PrefetchScalarGridSpec(
            num_scalar_prefetch=1,
            grid=(SHARE,),
            in_specs=[at(b) for b in range(N_SHOT)],
            out_specs=[pl.BlockSpec((1, CX, TY, AZ), lambda k, tile_of: (k, 0, 0, 0))] * 4,
        ),
        out_shape=[part] * 4,
    )(tile_of, *[slab] * 4)


def merge_kernel(used, *refs):
    out = refs[-1]
    slot = pl.program_id(0)
    for side in range(2):
        total = jnp.zeros((CX, TY, AZ), F32)
        for b in range(N_SHOT):
            part = refs[b][0]
            total = total + jnp.where(used[(b * SHARE + slot) * 2 + side] == 1, part, 0.0)
        out[side, 0] = total


def merge_tiles(used, bufs):
    spec = pl.BlockSpec((1, CX, TY, AZ), lambda k, *_: (k, 0, 0, 0))
    return pl.pallas_call(
        merge_kernel,
        grid_spec=pltpu.PrefetchScalarGridSpec(
            num_scalar_prefetch=1,
            grid=(SHARE,),
            in_specs=[spec] * len(bufs),
            out_specs=pl.BlockSpec((2, 1, CX, TY, AZ), lambda k, *_: (0, k, 0, 0, 0)),
        ),
        out_shape=sds((2, SHARE, CX, TY, AZ)),
        compiler_params=pltpu.CompilerParams(vmem_limit_bytes=VMEM),
    )(used, *bufs)


def within_shots(value, flip):
    return lax.ppermute(value, "shot", [(s, s ^ flip) for s in range(N_SHOT)])


def shift_column(value, amount, sign):
    def moved(value, steps):
        return lax.ppermute(value, "sub", [(j, (j + steps) % N_SUB) for j in range(N_SUB)])

    branches = [lambda v: v]
    for k in range(1, N_SUB):
        branches.append(functools.partial(moved, steps=sign * k))
    return lax.switch(amount, branches, value)


def exchange(low_planes, high_planes):
    up = [(i, i + 1) for i in range(N_SUB - 1)]
    down = [(b, a) for a, b in up]
    before = lax.ppermute(high_planes, "sub", up)
    after = lax.ppermute(low_planes, "sub", down)
    return before, after


def body(
    courant_tiles,
    tile_place,
    anchors,
    source_cells,
    wavelet,
    forward_state,
    adjoint_state,
    residual,
):
    my_shot = lax.axis_index("shot")
    my_sub = lax.axis_index("sub")
    start_x = anchors[:, 0]
    start_y = anchors[:, 1]
    amounts = start_x % N_SUB
    upper = (my_sub < start_x).astype(jnp.int32)
    column = my_sub + upper * N_SUB
    ids = start_y[:, None] + jnp.arange(KY, dtype=jnp.int32)[None, :]
    places = tile_place[column[:, None], ids]
    own_places = places[my_shot]

    pm, p0 = forward_state[0, 0], forward_state[0, 1]
    q5, q4 = adjoint_state[0, 0], adjoint_state[0, 1]

    bufs = []
    for flip in range(N_SHOT):
        mine = lax.dynamic_slice_in_dim(courant_tiles, upper[my_shot ^ flip] * SHARE, SHARE, 0)
        bufs.append(within_shots(mine, flip) if flip else mine)
    which = (own_places // SHARE) ^ my_shot
    slot = own_places % SHARE
    amount = amounts[my_shot]
    before, after = exchange(p0[0:R], p0[CX - R :])
    (lap0,) = run(lap_kernel, (), (p0, before, after), STENCIL, "s")

    cells = source_cells[my_shot] - jnp.stack([my_sub * CX, 0, 0]).astype(jnp.int32)
    amps = wavelet[0]
    source = (cells, amps)
    res = jnp.pad(
        residual[0].reshape(STEPS * CX, AY).T, ((0, 0), (0, AZ - STEPS * CX))
    )

    *bufs, lap0 = lax.optimization_barrier((*bufs, lap0))
    c = shift_column(pick_tiles(which, slot, bufs), amount, -1)
    p1, plo, phi, u, ulo, uhi = run(
        first_kernel, source, (p0, pm, lap0, q4, c), [BLOCK] * 5, "shhshh", stencil=False
    )
    ub, ua = exchange(ulo, uhi)
    pb, pa = exchange(plo, phi)
    q3, u, ulo, uhi = run(
        functools.partial(adjoint_kernel, 0),
        (),
        (u, ub, ua, q4, q5, c, res),
        STENCIL + [BLOCK] * 3 + [RES],
        "sshh",
    )
    ub, ua = exchange(ulo, uhi)
    lap1, p2, plo, phi = run(
        functools.partial(forward_kernel, 1),
        source,
        (p1, pb, pa, p0, c),
        STENCIL + [BLOCK] * 2,
        "sshh",
    )
    pb, pa = exchange(plo, phi)
    q2, u, ulo, uhi = run(
        functools.partial(adjoint_kernel, 1),
        (),
        (u, ub, ua, q3, q4, c, res),
        STENCIL + [BLOCK] * 3 + [RES],
        "sshh",
    )
    ub, ua = exchange(ulo, uhi)
    lap2, forward_out, plo, phi = run(
        third_forward_kernel, source, (p2, pb, pa, p1, c), STENCIL + [BLOCK] * 2, "s0hh"
    )
    pb, pa = exchange(plo, phi)
    adjoint_out, u, ulo, uhi, img = run(
        image_kernel,
        (),
        (u, ub, ua, q2, q3, c, res, lap2, lap1, lap0),
        STENCIL + [BLOCK] * 3 + [RES] + [BLOCK] * 3,
        "0shhs",
    )
    ub, ua = exchange(ulo, uhi)

    holder = jnp.arange(N_SHOT, dtype=jnp.int32)[:, None] ^ my_shot
    spot = holder * SHARE + jnp.arange(SHARE, dtype=jnp.int32)[None, :]
    match = spot.reshape(-1)[:, None] == own_places[None, :]
    tile_of = jnp.sum(
        jnp.where(match, jnp.arange(KY, dtype=jnp.int32)[None, :], 0), axis=1, dtype=jnp.int32
    )
    forward_out, grad = run(
        last_forward_kernel,
        source,
        (forward_out, pb, pa, p2, c, q4, img),
        [PAIR0_WHOLE, HBLOCK, HBLOCK] + [BLOCK] * 4,
        "1s",
        aliases={2: 0},
    )
    parts = pack_tiles(tile_of, shift_column(grad, amount, 1))
    got = [within_shots(part, flip) if flip else part for flip, part in enumerate(parts)]
    (adjoint_out,) = run(
        last_adjoint_kernel,
        (),
        (u, ub, ua, adjoint_out, q2, res),
        STENCIL + [PAIR0, BLOCK, RES],
        "1",
        aliases={3: 0},
    )
    *got, adjoint_out = lax.optimization_barrier((*got, adjoint_out))
    shots = jnp.arange(N_SHOT, dtype=jnp.int32) ^ my_shot
    mine = my_shot * SHARE + jnp.arange(SHARE, dtype=jnp.int32)
    covered = jnp.any(places[shots][:, None, :] == mine[None, :, None], axis=2)
    side = upper[shots][:, None, None] == jnp.arange(2, dtype=jnp.int32)[None, None, :]
    used = (covered[:, :, None] & side).astype(jnp.int32).reshape(-1)
    gradient_tiles = merge_tiles(used, got).reshape(courant_tiles.shape)

    return forward_out[None], adjoint_out[None], gradient_tiles


def solution(mesh):
    return jax.shard_map(
        body,
        mesh=mesh,
        in_specs=(
            P(("shot", "sub"), None, None, None),
            P(),
            P(),
            P(),
            P("shot", None),
            P("shot", None, "sub", None, None),
            P("shot", None, "sub", None, None),
            P("shot", None, "sub", None),
        ),
        out_specs=(
            P("shot", None, "sub", None, None),
            P("shot", None, "sub", None, None),
            P(("shot", "sub"), None, None, None),
        ),
        check_vma=False,
    )
```

```python
import functools

import jax
import jax.numpy as jnp
from jax import lax
from jax.experimental import pallas as pl
from jax.experimental.pallas import tpu as pltpu
from jax.sharding import PartitionSpec as P

CX = 6
TY = 64
AZ = 128
KY = 6
AY = KY * TY
STEPS = 4
N_SHOT = 4
N_SUB = 32
SHARE = 3
R = 4
PAD = 8

WEIGHTS = (1.6, -0.2, 8.0 / 315.0, -1.0 / 560.0)
CENTER = -205.0 / 72.0 * 3.0

F32 = jnp.float32
SLAB = (CX, AY, AZ)
HALO = (R, AY, AZ)
PAIR = (2, CX, AY, AZ)
BLOCK = pl.BlockSpec((CX, TY, AZ), lambda i, *_: (0, i, 0))
HBLOCK = pl.BlockSpec((R, TY, AZ), lambda i, *_: (0, i, 0))
WHOLE = pl.BlockSpec(SLAB, lambda i, *_: (0, 0, 0))
PAIR0 = pl.BlockSpec((1, CX, TY, AZ), lambda i, *_: (0, 0, i, 0))
PAIR1 = pl.BlockSpec((1, CX, TY, AZ), lambda i, *_: (1, 0, i, 0))
PAIR0_WHOLE = pl.BlockSpec((1, CX, AY, AZ), lambda i, *_: (0, 0, 0, 0))
RES = pl.BlockSpec((TY, AZ), lambda i, *_: (i, 0))
VMEM = 20 * 1024 * 1024


def sds(shape):
    return jax.ShapeDtypeStruct(shape, F32)


def fill_pad(src, pad):
    @pl.when(pl.program_id(0) == 0)
    def _():
        pad[:, 0:PAD, :] = jnp.zeros((CX, PAD, AZ), F32)
        pad[:, PAD + AY :, :] = jnp.zeros((CX, PAD, AZ), F32)
        pad[:, PAD : PAD + AY, :] = src[...]


def centre(x, base, pad):
    return pad[x, pl.ds(base + PAD, TY), :]


def laplacian(x, base, pad, lo, hi):
    def plane(k):
        if k < 0:
            return lo[k + R]
        if k >= CX:
            return hi[k - CX]
        return centre(k, base, pad)

    here = plane(x)
    lane = lax.broadcasted_iota(jnp.int32, (TY, AZ), 1)
    out = CENTER * here
    for r, w in enumerate(WEIGHTS, 1):
        out = out + w * (plane(x + r) + plane(x - r))
    for r, w in enumerate(WEIGHTS, 1):
        out = out + w * (
            pad[x, pl.ds(base + (PAD + r), TY), :] + pad[x, pl.ds(base + (PAD - r), TY), :]
        )
    for r, w in enumerate(WEIGHTS, 1):
        up = jnp.where(lane < AZ - r, pltpu.roll(here, AZ - r, 1), 0.0)
        down = jnp.where(lane >= r, pltpu.roll(here, r, 1), 0.0)
        out = out + w * (up + down)
    return out


def add_source(out, cells, amp, base):
    col = cells[1] - base
    inside = (cells[0] >= 0) & (cells[0] < CX) & (col >= 0) & (col < TY)

    @pl.when(inside)
    def _():
        lane = lax.broadcasted_iota(jnp.int32, (1, 1, AZ), 2)
        x = cells[0]
        row = out[pl.ds(x, 1), pl.ds(col, 1), :]
        out[pl.ds(x, 1), pl.ds(col, 1), :] = row + jnp.where(lane == cells[2], amp, 0.0)


def send_planes(value, lo, hi):
    lo[...] = value[0:R]
    hi[...] = value[CX - R :]


def block_base():
    return pl.multiple_of(pl.program_id(0) * TY, TY)


def first_kernel(cells, amps, src, lo, hi, old, q, c, lap, p1, plo, phi, u, ulo, uhi, pad):
    forward_kernel(0, cells, amps, src, lo, hi, old, c, lap, p1, plo, phi, pad)
    for x in range(CX):
        u[x] = c[x] * c[x] * q[x]
    send_planes(u, ulo, uhi)


def residual_term(step, x, res):
    lane = lax.broadcasted_iota(jnp.int32, (TY, AZ), 1)
    at = step * CX + x
    values = res[...]
    if at:
        values = pltpu.roll(values, AZ - at, 1)
    return jnp.where(lane == 0, values, 0.0)


def adjoint_kernel(step, src, lo, hi, now, old, c, res, new, u, ulo, uhi, pad):
    fill_pad(src, pad)
    for x in range(CX):
        curve = laplacian(x, block_base(), pad, lo, hi)
        value = 2.0 * now[x] - old[x] + curve + residual_term(step, x, res)
        new[x] = value
        u[x] = c[x] * c[x] * value
    send_planes(u, ulo, uhi)


def image_kernel(src, lo, hi, now, old, c, res, lap2, lap1, lap0, pair, u, ulo, uhi, img, pad):
    new = pair.at[0]
    adjoint_kernel(2, src, lo, hi, now, old, c, res, new, u, ulo, uhi, pad)
    for x in range(CX):
        img[x] = old[x] * lap2[x] + now[x] * lap1[x] + new[x] * lap0[x]


def last_adjoint_kernel(src, lo, hi, now, old, res, pair, pad):
    fill_pad(src, pad)
    for x in range(CX):
        curve = laplacian(x, block_base(), pad, lo, hi)
        pair[0, x] = 2.0 * now[0, x] - old[x] + curve + residual_term(3, x, res)


def forward_kernel(step, cells, amps, src, lo, hi, old, c, lap, new, nlo, nhi, pad):
    fill_pad(src, pad)
    base = block_base()
    for x in range(CX):
        curve = laplacian(x, base, pad, lo, hi)
        lap[x] = curve
        new[x] = 2.0 * centre(x, base, pad) - old[x] + c[x] * c[x] * curve
    add_source(new, cells, amps[step], base)
    send_planes(new, nlo, nhi)


def third_forward_kernel(cells, amps, src, lo, hi, old, c, lap, pair, nlo, nhi, pad):
    new = pair.at[0]
    forward_kernel(2, cells, amps, src, lo, hi, old, c, lap, new, nlo, nhi, pad)


def last_forward_kernel(cells, amps, src, lo, hi, old, c, q4, img, pair, grad, pad):
    fill_pad(src.at[0], pad)
    new = pair.at[0]
    base = block_base()
    for x in range(CX):
        curve = laplacian(x, base, pad, lo, hi)
        new[x] = 2.0 * centre(x, base, pad) - old[x] + c[x] * c[x] * curve
        grad[x] = 2.0 * c[x] * (img[x] + q4[x] * curve)
    add_source(new, cells, amps[3], base)


PAD_SCRATCH = pltpu.VMEM((CX, AY + 2 * PAD, AZ), F32)
OUTS = {
    "s": (SLAB, BLOCK),
    "h": (HALO, HBLOCK),
    "0": (PAIR, PAIR0),
    "1": (PAIR, PAIR1),
}


def size_of(shape):
    total = 4
    for n in shape:
        total *= n
    return total


def run(kernel, scalars, args, in_specs, outs, stencil=True, flops=10_000_000, aliases=None):
    kinds = [OUTS[k] for k in outs]
    traffic = sum(size_of(a.shape) for a in args) + sum(size_of(s) for s, _ in kinds)
    return pl.pallas_call(
        kernel,
        grid_spec=pltpu.PrefetchScalarGridSpec(
            num_scalar_prefetch=len(scalars),
            grid=(KY,),
            in_specs=in_specs,
            out_specs=[b for _, b in kinds],
            scratch_shapes=[PAD_SCRATCH] if stencil else [],
        ),
        out_shape=[sds(s) for s, _ in kinds],
        input_output_aliases=aliases or {},
        compiler_params=pltpu.CompilerParams(vmem_limit_bytes=VMEM),
        cost_estimate=pl.CostEstimate(flops=flops, bytes_accessed=traffic, transcendentals=0),
    )(*scalars, *args)


STENCIL = [WHOLE, HBLOCK, HBLOCK]


IN_VMEM = pl.BlockSpec(memory_space=pltpu.VMEM)
IN_SMEM = pl.BlockSpec(memory_space=pltpu.SMEM)


def pick_kernel(which, slot, b0, b1, b2, b3, out):
    for i in range(KY):
        for b, ref in enumerate((b0, b1, b2, b3)):

            @pl.when(which[i] == b)
            def _():
                out[:, i * TY : (i + 1) * TY, :] = ref[slot[i]]


def pick_tiles(which, slot, bufs):
    return pl.pallas_call(
        pick_kernel,
        in_specs=[IN_SMEM] * 2 + [IN_VMEM] * 4,
        out_specs=IN_VMEM,
        out_shape=sds(SLAB),
        compiler_params=pltpu.CompilerParams(vmem_limit_bytes=VMEM),
    )(which, slot, *bufs)


def pack_kernel(tile_of, slab, *outs):
    for b, out in enumerate(outs, 1):
        for k in range(SHARE):
            start = pl.multiple_of(tile_of[b * SHARE + k] * TY, TY)
            out[k] = slab[:, pl.ds(start, TY), :]


def pack_tiles(tile_of, slab):
    return pl.pallas_call(
        pack_kernel,
        in_specs=[IN_SMEM, IN_VMEM],
        out_specs=[IN_VMEM] * 3,
        out_shape=[sds((SHARE, CX, TY, AZ))] * 3,
        compiler_params=pltpu.CompilerParams(vmem_limit_bytes=VMEM),
    )(tile_of, slab)


def merge_kernel(used, tile_of, slab, b1, b2, b3, out):
    for slot in range(SHARE):
        start = pl.multiple_of(tile_of[slot] * TY, TY)
        for side in range(2):
            use = [used[(b * SHARE + slot) * 2 + side] == 1 for b in range(N_SHOT)]
            for x in range(CX):
                total = jnp.where(use[0], slab[x, pl.ds(start, TY), :], 0.0)
                for b, ref in enumerate((b1, b2, b3), 1):
                    total = total + jnp.where(use[b], ref[slot, x], 0.0)
                out[side * SHARE + slot, x] = total


def merge_tiles(used, tile_of, slab, bufs):
    return pl.pallas_call(
        merge_kernel,
        in_specs=[IN_SMEM] * 2 + [IN_VMEM] * 4,
        out_specs=IN_VMEM,
        out_shape=sds((2 * SHARE, CX, TY, AZ)),
        compiler_params=pltpu.CompilerParams(vmem_limit_bytes=VMEM),
    )(used, tile_of, slab, *bufs)


def within_shots(value, flip):
    return lax.ppermute(value, "shot", [(s, s ^ flip) for s in range(N_SHOT)])


def shift_column(value, amount, sign):
    def moved(value, steps):
        return lax.ppermute(value, "sub", [(j, (j + steps) % N_SUB) for j in range(N_SUB)])

    branches = [lambda v: v]
    for k in range(1, N_SUB):
        branches.append(functools.partial(moved, steps=sign * k))
    return lax.switch(amount, branches, value)


def exchange(low_planes, high_planes):
    up = [(i, i + 1) for i in range(N_SUB - 1)]
    down = [(b, a) for a, b in up]
    before = lax.ppermute(high_planes, "sub", up)
    after = lax.ppermute(low_planes, "sub", down)
    return before, after


def body(
    courant_tiles,
    tile_place,
    anchors,
    source_cells,
    wavelet,
    forward_state,
    adjoint_state,
    residual,
):
    my_shot = lax.axis_index("shot")
    my_sub = lax.axis_index("sub")
    start_x = anchors[:, 0]
    start_y = anchors[:, 1]
    amounts = start_x % N_SUB
    upper = (my_sub < start_x).astype(jnp.int32)
    column = my_sub + upper * N_SUB
    ids = start_y[:, None] + jnp.arange(KY, dtype=jnp.int32)[None, :]
    places = tile_place[column[:, None], ids]
    own_places = places[my_shot]

    pm, p0 = forward_state[0, 0], forward_state[0, 1]
    q5, q4 = adjoint_state[0, 0], adjoint_state[0, 1]

    mine = [
        lax.dynamic_slice_in_dim(courant_tiles, upper[my_shot ^ flip] * SHARE, SHARE, 0)
        for flip in range(N_SHOT)
    ]
    bufs = [mine[0]] + [within_shots(mine[flip], flip) for flip in range(1, N_SHOT)]
    which = (own_places // SHARE) ^ my_shot
    slot = own_places % SHARE
    amount = amounts[my_shot]
    bufs[1], low, high = lax.optimization_barrier((bufs[1], p0[0:R], p0[CX - R :]))
    before, after = exchange(low, high)

    cells = source_cells[my_shot] - jnp.stack([my_sub * CX, 0, 0]).astype(jnp.int32)
    amps = wavelet[0]
    source = (cells, amps)
    res = jnp.pad(
        residual[0].reshape(STEPS * CX, AY).T, ((0, 0), (0, AZ - STEPS * CX))
    )

    c = shift_column(pick_tiles(which, slot, bufs), amount, -1)
    lap0, p1, plo, phi, u, ulo, uhi = run(
        first_kernel, source, (p0, before, after, pm, q4, c), STENCIL + [BLOCK] * 3, "sshhshh"
    )
    ub, ua = exchange(ulo, uhi)
    pb, pa = exchange(plo, phi)
    q3, u, ulo, uhi = run(
        functools.partial(adjoint_kernel, 0),
        (),
        (u, ub, ua, q4, q5, c, res),
        STENCIL + [BLOCK] * 3 + [RES],
        "sshh",
    )
    ub, ua = exchange(ulo, uhi)
    lap1, p2, plo, phi = run(
        functools.partial(forward_kernel, 1),
        source,
        (p1, pb, pa, p0, c),
        STENCIL + [BLOCK] * 2,
        "sshh",
    )
    pb, pa = exchange(plo, phi)
    q2, u, ulo, uhi = run(
        functools.partial(adjoint_kernel, 1),
        (),
        (u, ub, ua, q3, q4, c, res),
        STENCIL + [BLOCK] * 3 + [RES],
        "sshh",
    )
    ub, ua = exchange(ulo, uhi)
    lap2, forward_out, plo, phi = run(
        third_forward_kernel, source, (p2, pb, pa, p1, c), STENCIL + [BLOCK] * 2, "s0hh"
    )
    pb, pa = exchange(plo, phi)
    adjoint_out, u, ulo, uhi, img = run(
        image_kernel,
        (),
        (u, ub, ua, q2, q3, c, res, lap2, lap1, lap0),
        STENCIL + [BLOCK] * 3 + [RES] + [BLOCK] * 3,
        "0shhs",
    )

    holder = jnp.arange(N_SHOT, dtype=jnp.int32)[:, None] ^ my_shot
    spot = holder * SHARE + jnp.arange(SHARE, dtype=jnp.int32)[None, :]
    match = spot.reshape(-1)[:, None] == own_places[None, :]
    tile_of = jnp.sum(
        jnp.where(match, jnp.arange(KY, dtype=jnp.int32)[None, :], 0), axis=1, dtype=jnp.int32
    )
    forward_out, grad = run(
        last_forward_kernel,
        source,
        (forward_out, pb, pa, p2, c, q4, img),
        [PAIR0_WHOLE, HBLOCK, HBLOCK] + [BLOCK] * 4,
        "1s",
        aliases={2: 0},
    )
    back = shift_column(grad, amount, 1)
    back, ulo, uhi = lax.optimization_barrier((back, ulo, uhi))
    ub, ua = exchange(ulo, uhi)
    parts = pack_tiles(tile_of, back)
    got = [within_shots(part, flip) for flip, part in enumerate(parts, 1)]
    (adjoint_out,) = run(
        last_adjoint_kernel,
        (),
        (u, ub, ua, adjoint_out, q2, res),
        STENCIL + [PAIR0, BLOCK, RES],
        "1",
        aliases={3: 0},
    )
    *got, adjoint_out = lax.optimization_barrier((*got, adjoint_out))
    shots = jnp.arange(N_SHOT, dtype=jnp.int32) ^ my_shot
    mine = my_shot * SHARE + jnp.arange(SHARE, dtype=jnp.int32)
    covered = jnp.any(places[shots][:, None, :] == mine[None, :, None], axis=2)
    side = upper[shots][:, None, None] == jnp.arange(2, dtype=jnp.int32)[None, None, :]
    used = (covered[:, :, None] & side).astype(jnp.int32).reshape(-1)
    gradient_tiles = merge_tiles(used, tile_of[:SHARE], back, got)

    return forward_out[None], adjoint_out[None], gradient_tiles


def solution(mesh):
    return jax.shard_map(
        body,
        mesh=mesh,
        in_specs=(
            P(("shot", "sub"), None, None, None),
            P(),
            P(),
            P(),
            P("shot", None),
            P("shot", None, "sub", None, None),
            P("shot", None, "sub", None, None),
            P("shot", None, "sub", None),
        ),
        out_specs=(
            P("shot", None, "sub", None, None),
            P("shot", None, "sub", None, None),
            P(("shot", "sub"), None, None, None),
        ),
        check_vma=False,
    )
```

```python
import functools

import jax
import jax.numpy as jnp
from jax import lax
from jax.experimental import pallas as pl
from jax.experimental.pallas import tpu as pltpu
from jax.sharding import PartitionSpec as P

CX = 6
TY = 64
AZ = 128
KY = 6
AY = KY * TY
STEPS = 4
N_SHOT = 4
N_SUB = 32
SHARE = 3
R = 4
PAD = 8

WEIGHTS = (1.6, -0.2, 8.0 / 315.0, -1.0 / 560.0)
CENTER = -205.0 / 72.0 * 3.0

F32 = jnp.float32
SLAB = (CX, AY, AZ)
HALO = (R, AY, AZ)
PAIR = (2, CX, AY, AZ)
BLOCK = pl.BlockSpec((CX, TY, AZ), lambda i, *_: (0, i, 0))
HBLOCK = pl.BlockSpec((R, TY, AZ), lambda i, *_: (0, i, 0))
WHOLE = pl.BlockSpec(SLAB, lambda i, *_: (0, 0, 0))
PAIR0 = pl.BlockSpec((1, CX, TY, AZ), lambda i, *_: (0, 0, i, 0))
PAIR1 = pl.BlockSpec((1, CX, TY, AZ), lambda i, *_: (1, 0, i, 0))
PAIR0_WHOLE = pl.BlockSpec((1, CX, AY, AZ), lambda i, *_: (0, 0, 0, 0))
RES = pl.BlockSpec((TY, AZ), lambda i, *_: (i, 0))
VMEM = 20 * 1024 * 1024


def sds(shape):
    return jax.ShapeDtypeStruct(shape, F32)


def fill_pad(src, pad):
    @pl.when(pl.program_id(0) == 0)
    def _():
        pad[:, 0:PAD, :] = jnp.zeros((CX, PAD, AZ), F32)
        pad[:, PAD + AY :, :] = jnp.zeros((CX, PAD, AZ), F32)
        pad[:, PAD : PAD + AY, :] = src[...]


def centre(x, base, pad):
    return pad[x, pl.ds(base + PAD, TY), :]


def laplacian(x, base, pad, lo, hi, ends):
    def plane(k):
        if k < 0:
            return jnp.where(ends[0] == 1, 0.0, lo[k + R])
        if k >= CX:
            return jnp.where(ends[1] == 1, 0.0, hi[k - CX])
        return centre(k, base, pad)

    here = plane(x)
    lane = lax.broadcasted_iota(jnp.int32, (TY, AZ), 1)
    out = CENTER * here
    for r, w in enumerate(WEIGHTS, 1):
        out = out + w * (plane(x + r) + plane(x - r))
    for r, w in enumerate(WEIGHTS, 1):
        out = out + w * (
            pad[x, pl.ds(base + (PAD + r), TY), :] + pad[x, pl.ds(base + (PAD - r), TY), :]
        )
    for r, w in enumerate(WEIGHTS, 1):
        up = jnp.where(lane < AZ - r, pltpu.roll(here, AZ - r, 1), 0.0)
        down = jnp.where(lane >= r, pltpu.roll(here, r, 1), 0.0)
        out = out + w * (up + down)
    return out


def add_source(out, cells, amp, base):
    col = cells[1] - base
    inside = (cells[0] >= 0) & (cells[0] < CX) & (col >= 0) & (col < TY)

    @pl.when(inside)
    def _():
        lane = lax.broadcasted_iota(jnp.int32, (1, 1, AZ), 2)
        x = cells[0]
        row = out[pl.ds(x, 1), pl.ds(col, 1), :]
        out[pl.ds(x, 1), pl.ds(col, 1), :] = row + jnp.where(lane == cells[2], amp, 0.0)


def send_planes(value, lo, hi):
    lo[...] = value[0:R]
    hi[...] = value[CX - R :]


def block_base():
    return pl.multiple_of(pl.program_id(0) * TY, TY)


def scale_kernel(c, q, u, ulo, uhi):
    for x in range(CX):
        u[x] = c[x] * c[x] * q[x]
    send_planes(u, ulo, uhi)


def residual_term(step, x, res):
    lane = lax.broadcasted_iota(jnp.int32, (TY, AZ), 1)
    at = step * CX + x
    values = res[...]
    if at:
        values = pltpu.roll(values, AZ - at, 1)
    return jnp.where(lane == 0, values, 0.0)


def adjoint_kernel(step, ends, src, lo, hi, now, old, c, res, new, u, ulo, uhi, pad):
    fill_pad(src, pad)
    for x in range(CX):
        curve = laplacian(x, block_base(), pad, lo, hi, ends)
        value = 2.0 * now[x] - old[x] + curve + residual_term(step, x, res)
        new[x] = value
        u[x] = c[x] * c[x] * value
    send_planes(u, ulo, uhi)


def image_kernel(ends, src, lo, hi, now, old, c, res, lap2, lap1, lap0, pair, u, ulo, uhi, img, pad):
    new = pair.at[0]
    adjoint_kernel(2, ends, src, lo, hi, now, old, c, res, new, u, ulo, uhi, pad)
    for x in range(CX):
        img[x] = old[x] * lap2[x] + now[x] * lap1[x] + new[x] * lap0[x]


def last_adjoint_kernel(ends, src, lo, hi, now, old, res, pair, pad):
    fill_pad(src, pad)
    for x in range(CX):
        curve = laplacian(x, block_base(), pad, lo, hi, ends)
        pair[0, x] = 2.0 * now[0, x] - old[x] + curve + residual_term(3, x, res)


def forward_kernel(step, ends, cells, amps, src, lo, hi, old, c, lap, new, nlo, nhi, pad):
    fill_pad(src, pad)
    base = block_base()
    for x in range(CX):
        curve = laplacian(x, base, pad, lo, hi, ends)
        lap[x] = curve
        new[x] = 2.0 * centre(x, base, pad) - old[x] + c[x] * c[x] * curve
    add_source(new, cells, amps[step], base)
    send_planes(new, nlo, nhi)


def third_forward_kernel(ends, cells, amps, src, lo, hi, old, c, lap, pair, nlo, nhi, pad):
    new = pair.at[0]
    forward_kernel(2, ends, cells, amps, src, lo, hi, old, c, lap, new, nlo, nhi, pad)


def last_forward_kernel(ends, cells, amps, src, lo, hi, old, c, q4, img, pair, grad, pad):
    fill_pad(src.at[0], pad)
    new = pair.at[0]
    base = block_base()
    for x in range(CX):
        curve = laplacian(x, base, pad, lo, hi, ends)
        new[x] = 2.0 * centre(x, base, pad) - old[x] + c[x] * c[x] * curve
        grad[x] = 2.0 * c[x] * (img[x] + q4[x] * curve)
    add_source(new, cells, amps[3], base)


PAD_SCRATCH = pltpu.VMEM((CX, AY + 2 * PAD, AZ), F32)
OUTS = {
    "s": (SLAB, BLOCK),
    "h": (HALO, HBLOCK),
    "0": (PAIR, PAIR0),
    "1": (PAIR, PAIR1),
}


def size_of(shape):
    total = 4
    for n in shape:
        total *= n
    return total


def run(kernel, scalars, args, in_specs, outs, stencil=True, flops=10_000_000, aliases=None):
    kinds = [OUTS[k] for k in outs]
    traffic = sum(size_of(a.shape) for a in args) + sum(size_of(s) for s, _ in kinds)
    return pl.pallas_call(
        kernel,
        grid_spec=pltpu.PrefetchScalarGridSpec(
            num_scalar_prefetch=len(scalars),
            grid=(KY,),
            in_specs=in_specs,
            out_specs=[b for _, b in kinds],
            scratch_shapes=[PAD_SCRATCH] if stencil else [],
        ),
        out_shape=[sds(s) for s, _ in kinds],
        input_output_aliases=aliases or {},
        compiler_params=pltpu.CompilerParams(vmem_limit_bytes=VMEM),
        cost_estimate=pl.CostEstimate(flops=flops, bytes_accessed=traffic, transcendentals=0),
    )(*scalars, *args)


STENCIL = [WHOLE, HBLOCK, HBLOCK]


IN_VMEM = pl.BlockSpec(memory_space=pltpu.VMEM)
IN_SMEM = pl.BlockSpec(memory_space=pltpu.SMEM)


def pick_kernel(which, slot, b0, b1, b2, b3, out):
    for i in range(KY):
        for b, ref in enumerate((b0, b1, b2, b3)):

            @pl.when(which[i] == b)
            def _():
                out[:, i * TY : (i + 1) * TY, :] = ref[slot[i]]


def pick_tiles(which, slot, bufs):
    return pl.pallas_call(
        pick_kernel,
        in_specs=[IN_SMEM] * 2 + [IN_VMEM] * 4,
        out_specs=IN_VMEM,
        out_shape=sds(SLAB),
        compiler_params=pltpu.CompilerParams(vmem_limit_bytes=VMEM),
    )(which, slot, *bufs)


def pack_kernel(tile_of, slab, *outs):
    for b, out in enumerate(outs, 1):
        for k in range(SHARE):
            start = pl.multiple_of(tile_of[b * SHARE + k] * TY, TY)
            out[k] = slab[:, pl.ds(start, TY), :]


def pack_tiles(tile_of, slab):
    return pl.pallas_call(
        pack_kernel,
        in_specs=[IN_SMEM, IN_VMEM],
        out_specs=[IN_VMEM] * 3,
        out_shape=[sds((SHARE, CX, TY, AZ))] * 3,
        compiler_params=pltpu.CompilerParams(vmem_limit_bytes=VMEM),
    )(tile_of, slab)


def merge_kernel(used, tile_of, slab, b1, b2, b3, out):
    for slot in range(SHARE):
        start = pl.multiple_of(tile_of[slot] * TY, TY)
        for side in range(2):
            use = [used[(b * SHARE + slot) * 2 + side] == 1 for b in range(N_SHOT)]
            for x in range(CX):
                total = jnp.where(use[0], slab[x, pl.ds(start, TY), :], 0.0)
                for b, ref in enumerate((b1, b2, b3), 1):
                    total = total + jnp.where(use[b], ref[slot, x], 0.0)
                out[side * SHARE + slot, x] = total


def merge_tiles(used, tile_of, slab, bufs):
    return pl.pallas_call(
        merge_kernel,
        in_specs=[IN_SMEM] * 2 + [IN_VMEM] * 4,
        out_specs=IN_VMEM,
        out_shape=sds((2 * SHARE, CX, TY, AZ)),
        compiler_params=pltpu.CompilerParams(vmem_limit_bytes=VMEM),
    )(used, tile_of, slab, *bufs)


def within_shots(value, flip):
    return lax.ppermute(value, "shot", [(s, s ^ flip) for s in range(N_SHOT)])


def shift_column(value, amount, sign):
    def moved(value, steps):
        return lax.ppermute(value, "sub", [(j, (j + steps) % N_SUB) for j in range(N_SUB)])

    branches = [lambda v: v]
    for k in range(1, N_SUB):
        branches.append(functools.partial(moved, steps=sign * k))
    return lax.switch(amount, branches, value)


def exchange(low_planes, high_planes):
    up = [(i, (i + 1) % N_SUB) for i in range(N_SUB)]
    down = [(i, (i - 1) % N_SUB) for i in range(N_SUB)]
    before = lax.ppermute(high_planes, "sub", up)
    after = lax.ppermute(low_planes, "sub", down)
    return before, after


def body(
    courant_tiles,
    tile_place,
    anchors,
    source_cells,
    wavelet,
    forward_state,
    adjoint_state,
    residual,
):
    my_shot = lax.axis_index("shot")
    my_sub = lax.axis_index("sub")
    start_x = anchors[:, 0]
    start_y = anchors[:, 1]
    amounts = start_x % N_SUB
    upper = (my_sub < start_x).astype(jnp.int32)
    column = my_sub + upper * N_SUB
    ids = start_y[:, None] + jnp.arange(KY, dtype=jnp.int32)[None, :]
    places = tile_place[column[:, None], ids]
    own_places = places[my_shot]

    pm, p0 = forward_state[0, 0], forward_state[0, 1]
    q5, q4 = adjoint_state[0, 0], adjoint_state[0, 1]

    mine = [
        lax.dynamic_slice_in_dim(courant_tiles, upper[my_shot ^ flip] * SHARE, SHARE, 0)
        for flip in range(N_SHOT)
    ]
    bufs = [mine[0]] + [within_shots(mine[flip], flip) for flip in range(1, N_SHOT)]
    which = (own_places // SHARE) ^ my_shot
    slot = own_places % SHARE
    amount = amounts[my_shot]
    cells = source_cells[my_shot] - jnp.stack([my_sub * CX, 0, 0]).astype(jnp.int32)
    amps = wavelet[0]
    ends = jnp.stack([my_sub == 0, my_sub == N_SUB - 1]).astype(jnp.int32)
    source = (ends, cells, amps)
    res = jnp.pad(
        residual[0].reshape(STEPS * CX, AY).T, ((0, 0), (0, AZ - STEPS * CX))
    )

    c = shift_column(pick_tiles(which, slot, bufs), amount, -1)
    c, low, high = lax.optimization_barrier((c, p0[0:R], p0[CX - R :]))
    before, after = exchange(low, high)
    u, ulo, uhi = run(scale_kernel, (), (c, q4), [BLOCK] * 2, "shh", stencil=False)
    ub, ua = exchange(ulo, uhi)
    lap0, p1, plo, phi = run(
        functools.partial(forward_kernel, 0),
        source,
        (p0, before, after, pm, c),
        STENCIL + [BLOCK] * 2,
        "sshh",
    )
    pb, pa = exchange(plo, phi)
    q3, u, ulo, uhi = run(
        functools.partial(adjoint_kernel, 0),
        (ends,),
        (u, ub, ua, q4, q5, c, res),
        STENCIL + [BLOCK] * 3 + [RES],
        "sshh",
    )
    ub, ua = exchange(ulo, uhi)
    lap1, p2, plo, phi = run(
        functools.partial(forward_kernel, 1),
        source,
        (p1, pb, pa, p0, c),
        STENCIL + [BLOCK] * 2,
        "sshh",
    )
    pb, pa = exchange(plo, phi)
    q2, u, ulo, uhi = run(
        functools.partial(adjoint_kernel, 1),
        (ends,),
        (u, ub, ua, q3, q4, c, res),
        STENCIL + [BLOCK] * 3 + [RES],
        "sshh",
    )
    ub, ua = exchange(ulo, uhi)
    lap2, forward_out, plo, phi = run(
        third_forward_kernel, source, (p2, pb, pa, p1, c), STENCIL + [BLOCK] * 2, "s0hh"
    )
    pb, pa = exchange(plo, phi)
    adjoint_out, u, ulo, uhi, img = run(
        image_kernel,
        (ends,),
        (u, ub, ua, q2, q3, c, res, lap2, lap1, lap0),
        STENCIL + [BLOCK] * 3 + [RES] + [BLOCK] * 3,
        "0shhs",
    )
    ub, ua = exchange(ulo, uhi)

    holder = jnp.arange(N_SHOT, dtype=jnp.int32)[:, None] ^ my_shot
    spot = holder * SHARE + jnp.arange(SHARE, dtype=jnp.int32)[None, :]
    match = spot.reshape(-1)[:, None] == own_places[None, :]
    tile_of = jnp.sum(
        jnp.where(match, jnp.arange(KY, dtype=jnp.int32)[None, :], 0), axis=1, dtype=jnp.int32
    )
    forward_out, grad = run(
        last_forward_kernel,
        source,
        (forward_out, pb, pa, p2, c, q4, img),
        [PAIR0_WHOLE, HBLOCK, HBLOCK] + [BLOCK] * 4,
        "1s",
        aliases={3: 0},
    )
    back = shift_column(grad, amount, 1)
    parts = pack_tiles(tile_of, back)
    got = [within_shots(part, flip) for flip, part in enumerate(parts, 1)]
    (adjoint_out,) = run(
        last_adjoint_kernel,
        (ends,),
        (u, ub, ua, adjoint_out, q2, res),
        STENCIL + [PAIR0, BLOCK, RES],
        "1",
        aliases={4: 0},
    )
    *got, adjoint_out = lax.optimization_barrier((*got, adjoint_out))
    shots = jnp.arange(N_SHOT, dtype=jnp.int32) ^ my_shot
    mine = my_shot * SHARE + jnp.arange(SHARE, dtype=jnp.int32)
    covered = jnp.any(places[shots][:, None, :] == mine[None, :, None], axis=2)
    side = upper[shots][:, None, None] == jnp.arange(2, dtype=jnp.int32)[None, None, :]
    used = (covered[:, :, None] & side).astype(jnp.int32).reshape(-1)
    gradient_tiles = merge_tiles(used, tile_of[:SHARE], back, got)

    return forward_out[None], adjoint_out[None], gradient_tiles


def solution(mesh):
    return jax.shard_map(
        body,
        mesh=mesh,
        in_specs=(
            P(("shot", "sub"), None, None, None),
            P(),
            P(),
            P(),
            P("shot", None),
            P("shot", None, "sub", None, None),
            P("shot", None, "sub", None, None),
            P("shot", None, "sub", None),
        ),
        out_specs=(
            P("shot", None, "sub", None, None),
            P("shot", None, "sub", None, None),
            P(("shot", "sub"), None, None, None),
        ),
        check_vma=False,
    )
```

```python
import functools

import jax
import jax.numpy as jnp
from jax import lax
from jax.experimental import pallas as pl
from jax.experimental.pallas import tpu as pltpu
from jax.sharding import PartitionSpec as P

CX = 6
TY = 64
AZ = 128
KY = 6
AY = KY * TY
STEPS = 4
N_SHOT = 4
N_SUB = 32
SHARE = 3
R = 4
PAD = 8

WEIGHTS = (1.6, -0.2, 8.0 / 315.0, -1.0 / 560.0)
CENTER = -205.0 / 72.0 * 3.0

F32 = jnp.float32
SLAB = (CX, AY, AZ)
HALO = (R, AY, AZ)
PAIR = (2, CX, AY, AZ)
BLOCK = pl.BlockSpec((CX, TY, AZ), lambda i, *_: (0, i, 0))
HBLOCK = pl.BlockSpec((R, TY, AZ), lambda i, *_: (0, i, 0))
WHOLE = pl.BlockSpec(SLAB, lambda i, *_: (0, 0, 0))
PAIR0 = pl.BlockSpec((1, CX, TY, AZ), lambda i, *_: (0, 0, i, 0))
PAIR1 = pl.BlockSpec((1, CX, TY, AZ), lambda i, *_: (1, 0, i, 0))
PAIR0_WHOLE = pl.BlockSpec((1, CX, AY, AZ), lambda i, *_: (0, 0, 0, 0))
RES = pl.BlockSpec((TY, AZ), lambda i, *_: (i, 0))
VMEM = 20 * 1024 * 1024


def sds(shape):
    return jax.ShapeDtypeStruct(shape, F32)


def fill_pad(src, pad):
    @pl.when(pl.program_id(0) == 0)
    def _():
        pad[:, 0:PAD, :] = jnp.zeros((CX, PAD, AZ), F32)
        pad[:, PAD + AY :, :] = jnp.zeros((CX, PAD, AZ), F32)
        pad[:, PAD : PAD + AY, :] = src[...]


def centre(x, base, pad):
    return pad[x, pl.ds(base + PAD, TY), :]


def laplacian(x, base, pad, lo, hi, ends):
    def plane(k):
        if k < 0:
            return jnp.where(ends[0] == 1, 0.0, lo[k + R])
        if k >= CX:
            return jnp.where(ends[1] == 1, 0.0, hi[k - CX])
        return centre(k, base, pad)

    here = plane(x)
    lane = lax.broadcasted_iota(jnp.int32, (TY, AZ), 1)
    out = CENTER * here
    for r, w in enumerate(WEIGHTS, 1):
        out = out + w * (plane(x + r) + plane(x - r))
    for r, w in enumerate(WEIGHTS, 1):
        out = out + w * (
            pad[x, pl.ds(base + (PAD + r), TY), :] + pad[x, pl.ds(base + (PAD - r), TY), :]
        )
    for r, w in enumerate(WEIGHTS, 1):
        up = jnp.where(lane < AZ - r, pltpu.roll(here, AZ - r, 1), 0.0)
        down = jnp.where(lane >= r, pltpu.roll(here, r, 1), 0.0)
        out = out + w * (up + down)
    return out


def add_source(out, cells, amp, base):
    col = cells[1] - base
    inside = (cells[0] >= 0) & (cells[0] < CX) & (col >= 0) & (col < TY)

    @pl.when(inside)
    def _():
        lane = lax.broadcasted_iota(jnp.int32, (1, 1, AZ), 2)
        x = cells[0]
        row = out[pl.ds(x, 1), pl.ds(col, 1), :]
        out[pl.ds(x, 1), pl.ds(col, 1), :] = row + jnp.where(lane == cells[2], amp, 0.0)


def send_planes(value, lo, hi):
    lo[...] = value[0:R]
    hi[...] = value[CX - R :]


def block_base():
    return pl.multiple_of(pl.program_id(0) * TY, TY)


def scale_kernel(c, q, u, ulo, uhi):
    for x in range(CX):
        u[x] = c[x] * c[x] * q[x]
    send_planes(u, ulo, uhi)


def residual_term(step, x, res):
    lane = lax.broadcasted_iota(jnp.int32, (TY, AZ), 1)
    at = step * CX + x
    values = res[...]
    if at:
        values = pltpu.roll(values, AZ - at, 1)
    return jnp.where(lane == 0, values, 0.0)


def adjoint_kernel(step, ends, src, lo, hi, now, old, c, res, new, u, ulo, uhi, pad):
    fill_pad(src, pad)
    for x in range(CX):
        curve = laplacian(x, block_base(), pad, lo, hi, ends)
        value = 2.0 * now[x] - old[x] + curve + residual_term(step, x, res)
        new[x] = value
        u[x] = c[x] * c[x] * value
    send_planes(u, ulo, uhi)


def middle_adjoint_kernel(ends, src, lo, hi, now, old, c, res, lap1, new, u, ulo, uhi, img, pad):
    adjoint_kernel(1, ends, src, lo, hi, now, old, c, res, new, u, ulo, uhi, pad)
    for x in range(CX):
        img[x] = new[x] * lap1[x]


def image_kernel(ends, src, lo, hi, now, old, c, res, part, lap0, pair, u, ulo, uhi, img, pad):
    new = pair.at[0]
    adjoint_kernel(2, ends, src, lo, hi, now, old, c, res, new, u, ulo, uhi, pad)
    for x in range(CX):
        img[x] = part[x] + new[x] * lap0[x]


def last_adjoint_kernel(ends, src, lo, hi, now, old, res, pair, pad):
    fill_pad(src, pad)
    for x in range(CX):
        curve = laplacian(x, block_base(), pad, lo, hi, ends)
        pair[0, x] = 2.0 * now[0, x] - old[x] + curve + residual_term(3, x, res)


def forward_kernel(step, ends, cells, amps, src, lo, hi, old, c, lap, new, nlo, nhi, pad):
    fill_pad(src, pad)
    base = block_base()
    for x in range(CX):
        curve = laplacian(x, base, pad, lo, hi, ends)
        lap[x] = curve
        new[x] = 2.0 * centre(x, base, pad) - old[x] + c[x] * c[x] * curve
    add_source(new, cells, amps[step], base)
    send_planes(new, nlo, nhi)


def third_forward_kernel(
    ends, cells, amps, src, lo, hi, old, c, q3, part, img, pair, nlo, nhi, pad
):
    new = pair.at[0]
    forward_kernel(2, ends, cells, amps, src, lo, hi, old, c, img, new, nlo, nhi, pad)
    for x in range(CX):
        img[x] = part[x] + q3[x] * img[x]


def last_forward_kernel(ends, cells, amps, src, lo, hi, old, c, q4, img, pair, grad, pad):
    fill_pad(src.at[0], pad)
    new = pair.at[0]
    base = block_base()
    for x in range(CX):
        curve = laplacian(x, base, pad, lo, hi, ends)
        new[x] = 2.0 * centre(x, base, pad) - old[x] + c[x] * c[x] * curve
        grad[x] = 2.0 * c[x] * (img[x] + q4[x] * curve)
    add_source(new, cells, amps[3], base)


PAD_SCRATCH = pltpu.VMEM((CX, AY + 2 * PAD, AZ), F32)
OUTS = {
    "s": (SLAB, BLOCK),
    "h": (HALO, HBLOCK),
    "0": (PAIR, PAIR0),
    "1": (PAIR, PAIR1),
}


def size_of(shape):
    total = 4
    for n in shape:
        total *= n
    return total


def run(kernel, scalars, args, in_specs, outs, stencil=True, flops=10_000_000, aliases=None):
    kinds = [OUTS[k] for k in outs]
    traffic = sum(size_of(a.shape) for a in args) + sum(size_of(s) for s, _ in kinds)
    return pl.pallas_call(
        kernel,
        grid_spec=pltpu.PrefetchScalarGridSpec(
            num_scalar_prefetch=len(scalars),
            grid=(KY,),
            in_specs=in_specs,
            out_specs=[b for _, b in kinds],
            scratch_shapes=[PAD_SCRATCH] if stencil else [],
        ),
        out_shape=[sds(s) for s, _ in kinds],
        input_output_aliases=aliases or {},
        compiler_params=pltpu.CompilerParams(vmem_limit_bytes=VMEM),
        cost_estimate=pl.CostEstimate(flops=flops, bytes_accessed=traffic, transcendentals=0),
    )(*scalars, *args)


STENCIL = [WHOLE, HBLOCK, HBLOCK]


IN_VMEM = pl.BlockSpec(memory_space=pltpu.VMEM)
IN_SMEM = pl.BlockSpec(memory_space=pltpu.SMEM)


def pick_kernel(which, slot, b0, b1, b2, b3, out):
    for i in range(KY):
        for b, ref in enumerate((b0, b1, b2, b3)):

            @pl.when(which[i] == b)
            def _():
                out[:, i * TY : (i + 1) * TY, :] = ref[slot[i]]


def pick_tiles(which, slot, bufs):
    return pl.pallas_call(
        pick_kernel,
        in_specs=[IN_SMEM] * 2 + [IN_VMEM] * 4,
        out_specs=IN_VMEM,
        out_shape=sds(SLAB),
        compiler_params=pltpu.CompilerParams(vmem_limit_bytes=VMEM),
    )(which, slot, *bufs)


def pack_kernel(tile_of, slab, *outs):
    for b, out in enumerate(outs, 1):
        for k in range(SHARE):
            start = pl.multiple_of(tile_of[b * SHARE + k] * TY, TY)
            out[k] = slab[:, pl.ds(start, TY), :]


def pack_tiles(tile_of, slab):
    return pl.pallas_call(
        pack_kernel,
        in_specs=[IN_SMEM, IN_VMEM],
        out_specs=[IN_VMEM] * 3,
        out_shape=[sds((SHARE, CX, TY, AZ))] * 3,
        compiler_params=pltpu.CompilerParams(vmem_limit_bytes=VMEM),
    )(tile_of, slab)


def merge_kernel(used, tile_of, slab, b1, b2, b3, out):
    for slot in range(SHARE):
        start = pl.multiple_of(tile_of[slot] * TY, TY)
        for side in range(2):
            use = [used[(b * SHARE + slot) * 2 + side] == 1 for b in range(N_SHOT)]
            for x in range(CX):
                total = jnp.where(use[0], slab[x, pl.ds(start, TY), :], 0.0)
                for b, ref in enumerate((b1, b2, b3), 1):
                    total = total + jnp.where(use[b], ref[slot, x], 0.0)
                out[side * SHARE + slot, x] = total


def merge_tiles(used, tile_of, slab, bufs):
    return pl.pallas_call(
        merge_kernel,
        in_specs=[IN_SMEM] * 2 + [IN_VMEM] * 4,
        out_specs=IN_VMEM,
        out_shape=sds((2 * SHARE, CX, TY, AZ)),
        compiler_params=pltpu.CompilerParams(vmem_limit_bytes=VMEM),
    )(used, tile_of, slab, *bufs)


def within_shots(value, flip):
    return lax.ppermute(value, "shot", [(s, s ^ flip) for s in range(N_SHOT)])


def shift_column(value, amount, sign):
    def moved(value, steps):
        return lax.ppermute(value, "sub", [(j, (j + steps) % N_SUB) for j in range(N_SUB)])

    branches = [lambda v: v]
    for k in range(1, N_SUB):
        branches.append(functools.partial(moved, steps=sign * k))
    return lax.switch(amount, branches, value)


def exchange(low_planes, high_planes):
    up = [(i, (i + 1) % N_SUB) for i in range(N_SUB)]
    down = [(i, (i - 1) % N_SUB) for i in range(N_SUB)]
    before = lax.ppermute(high_planes, "sub", up)
    after = lax.ppermute(low_planes, "sub", down)
    return before, after


def body(
    courant_tiles,
    tile_place,
    anchors,
    source_cells,
    wavelet,
    forward_state,
    adjoint_state,
    residual,
):
    my_shot = lax.axis_index("shot")
    my_sub = lax.axis_index("sub")
    start_x = anchors[:, 0]
    start_y = anchors[:, 1]
    amounts = start_x % N_SUB
    upper = (my_sub < start_x).astype(jnp.int32)
    column = my_sub + upper * N_SUB
    ids = start_y[:, None] + jnp.arange(KY, dtype=jnp.int32)[None, :]
    places = tile_place[column[:, None], ids]
    own_places = places[my_shot]

    pm, p0 = forward_state[0, 0], forward_state[0, 1]
    q5, q4 = adjoint_state[0, 0], adjoint_state[0, 1]

    mine = [
        lax.dynamic_slice_in_dim(courant_tiles, upper[my_shot ^ flip] * SHARE, SHARE, 0)
        for flip in range(N_SHOT)
    ]
    bufs = [mine[0]] + [within_shots(mine[flip], flip) for flip in range(1, N_SHOT)]
    which = (own_places // SHARE) ^ my_shot
    slot = own_places % SHARE
    amount = amounts[my_shot]
    cells = source_cells[my_shot] - jnp.stack([my_sub * CX, 0, 0]).astype(jnp.int32)
    amps = wavelet[0]
    ends = jnp.stack([my_sub == 0, my_sub == N_SUB - 1]).astype(jnp.int32)
    source = (ends, cells, amps)
    res = jnp.pad(
        residual[0].reshape(STEPS * CX, AY).T, ((0, 0), (0, AZ - STEPS * CX))
    )

    c = shift_column(pick_tiles(which, slot, bufs), amount, -1)
    c, low, high = lax.optimization_barrier((c, p0[0:R], p0[CX - R :]))
    before, after = exchange(low, high)
    u, ulo, uhi = run(scale_kernel, (), (c, q4), [BLOCK] * 2, "shh", stencil=False)
    ub, ua = exchange(ulo, uhi)
    lap0, p1, plo, phi = run(
        functools.partial(forward_kernel, 0),
        source,
        (p0, before, after, pm, c),
        STENCIL + [BLOCK] * 2,
        "sshh",
    )
    pb, pa = exchange(plo, phi)
    q3, u, ulo, uhi = run(
        functools.partial(adjoint_kernel, 0),
        (ends,),
        (u, ub, ua, q4, q5, c, res),
        STENCIL + [BLOCK] * 3 + [RES],
        "sshh",
    )
    ub, ua = exchange(ulo, uhi)
    lap1, p2, plo, phi = run(
        functools.partial(forward_kernel, 1),
        source,
        (p1, pb, pa, p0, c),
        STENCIL + [BLOCK] * 2,
        "sshh",
    )
    pb, pa = exchange(plo, phi)
    q2, u, ulo, uhi, img = run(
        middle_adjoint_kernel,
        (ends,),
        (u, ub, ua, q3, q4, c, res, lap1),
        STENCIL + [BLOCK] * 3 + [RES, BLOCK],
        "sshhs",
    )
    ub, ua = exchange(ulo, uhi)
    img, forward_out, plo, phi = run(
        third_forward_kernel,
        source,
        (p2, pb, pa, p1, c, q3, img),
        STENCIL + [BLOCK] * 4,
        "s0hh",
    )
    pb, pa = exchange(plo, phi)
    adjoint_out, u, ulo, uhi, img = run(
        image_kernel,
        (ends,),
        (u, ub, ua, q2, q3, c, res, img, lap0),
        STENCIL + [BLOCK] * 3 + [RES] + [BLOCK] * 2,
        "0shhs",
    )
    ub, ua = exchange(ulo, uhi)

    holder = jnp.arange(N_SHOT, dtype=jnp.int32)[:, None] ^ my_shot
    spot = holder * SHARE + jnp.arange(SHARE, dtype=jnp.int32)[None, :]
    match = spot.reshape(-1)[:, None] == own_places[None, :]
    tile_of = jnp.sum(
        jnp.where(match, jnp.arange(KY, dtype=jnp.int32)[None, :], 0), axis=1, dtype=jnp.int32
    )
    forward_out, grad = run(
        last_forward_kernel,
        source,
        (forward_out, pb, pa, p2, c, q4, img),
        [PAIR0_WHOLE, HBLOCK, HBLOCK] + [BLOCK] * 4,
        "1s",
        aliases={3: 0},
    )
    back = shift_column(grad, amount, 1)
    parts = pack_tiles(tile_of, back)
    got = [within_shots(part, flip) for flip, part in enumerate(parts, 1)]
    (adjoint_out,) = run(
        last_adjoint_kernel,
        (ends,),
        (u, ub, ua, adjoint_out, q2, res),
        STENCIL + [PAIR0, BLOCK, RES],
        "1",
        aliases={4: 0},
    )
    *got, adjoint_out = lax.optimization_barrier((*got, adjoint_out))
    shots = jnp.arange(N_SHOT, dtype=jnp.int32) ^ my_shot
    mine = my_shot * SHARE + jnp.arange(SHARE, dtype=jnp.int32)
    covered = jnp.any(places[shots][:, None, :] == mine[None, :, None], axis=2)
    side = upper[shots][:, None, None] == jnp.arange(2, dtype=jnp.int32)[None, None, :]
    used = (covered[:, :, None] & side).astype(jnp.int32).reshape(-1)
    gradient_tiles = merge_tiles(used, tile_of[:SHARE], back, got)

    return forward_out[None], adjoint_out[None], gradient_tiles


def solution(mesh):
    return jax.shard_map(
        body,
        mesh=mesh,
        in_specs=(
            P(("shot", "sub"), None, None, None),
            P(),
            P(),
            P(),
            P("shot", None),
            P("shot", None, "sub", None, None),
            P("shot", None, "sub", None, None),
            P("shot", None, "sub", None),
        ),
        out_specs=(
            P("shot", None, "sub", None, None),
            P("shot", None, "sub", None, None),
            P(("shot", "sub"), None, None, None),
        ),
        check_vma=False,
    )
```

```python
import functools

import jax
import jax.numpy as jnp
from jax import lax
from jax.experimental import pallas as pl
from jax.experimental.pallas import tpu as pltpu
from jax.sharding import PartitionSpec as P

CX = 6
TY = 64
AZ = 128
KY = 6
AY = KY * TY
STEPS = 4
N_SHOT = 4
N_SUB = 32
SHARE = 3
R = 4
PAD = 8

WEIGHTS = (1.6, -0.2, 8.0 / 315.0, -1.0 / 560.0)
CENTER = -205.0 / 72.0 * 3.0

F32 = jnp.float32
SLAB = (CX, AY, AZ)
HALO = (R, AY, AZ)
PAIR = (2, CX, AY, AZ)
BLOCK = pl.BlockSpec((CX, TY, AZ), lambda i, *_: (0, i, 0))
HBLOCK = pl.BlockSpec((R, TY, AZ), lambda i, *_: (0, i, 0))
WHOLE = pl.BlockSpec(SLAB, lambda i, *_: (0, 0, 0))
PAIR0 = pl.BlockSpec((1, CX, TY, AZ), lambda i, *_: (0, 0, i, 0))
PAIR1 = pl.BlockSpec((1, CX, TY, AZ), lambda i, *_: (1, 0, i, 0))
PAIR0_WHOLE = pl.BlockSpec((1, CX, AY, AZ), lambda i, *_: (0, 0, 0, 0))
RES = pl.BlockSpec((TY, AZ), lambda i, *_: (i, 0))
VMEM = 20 * 1024 * 1024


def sds(shape):
    return jax.ShapeDtypeStruct(shape, F32)


def fill_pad(src, pad):
    @pl.when(pl.program_id(0) == 0)
    def _():
        pad[:, 0:PAD, :] = jnp.zeros((CX, PAD, AZ), F32)
        pad[:, PAD + AY :, :] = jnp.zeros((CX, PAD, AZ), F32)
        pad[:, PAD : PAD + AY, :] = src[...]


def centre(x, base, pad):
    return pad[x, pl.ds(base + PAD, TY), :]


def laplacian(x, base, pad, lo, hi, ends):
    def plane(k):
        if k < 0:
            return jnp.where(ends[0] == 1, 0.0, lo[k + R])
        if k >= CX:
            return jnp.where(ends[1] == 1, 0.0, hi[k - CX])
        return centre(k, base, pad)

    here = plane(x)
    lane = lax.broadcasted_iota(jnp.int32, (TY, AZ), 1)
    out = CENTER * here
    for r, w in enumerate(WEIGHTS, 1):
        out = out + w * (plane(x + r) + plane(x - r))
    for r, w in enumerate(WEIGHTS, 1):
        out = out + w * (
            pad[x, pl.ds(base + (PAD + r), TY), :] + pad[x, pl.ds(base + (PAD - r), TY), :]
        )
    for r, w in enumerate(WEIGHTS, 1):
        up = jnp.where(lane < AZ - r, pltpu.roll(here, AZ - r, 1), 0.0)
        down = jnp.where(lane >= r, pltpu.roll(here, r, 1), 0.0)
        out = out + w * (up + down)
    return out


def add_source(out, cells, amp, base):
    col = cells[1] - base
    inside = (cells[0] >= 0) & (cells[0] < CX) & (col >= 0) & (col < TY)

    @pl.when(inside)
    def _():
        lane = lax.broadcasted_iota(jnp.int32, (1, 1, AZ), 2)
        x = cells[0]
        row = out[pl.ds(x, 1), pl.ds(col, 1), :]
        out[pl.ds(x, 1), pl.ds(col, 1), :] = row + jnp.where(lane == cells[2], amp, 0.0)


def send_planes(value, lo, hi):
    lo[...] = value[0:R]
    hi[...] = value[CX - R :]


def block_base():
    return pl.multiple_of(pl.program_id(0) * TY, TY)


def rest_kernel(now, old, rest):
    for x in range(CX):
        rest[x] = 2.0 * now[x] - old[x]


def first_forward_kernel(ends, cells, amps, src, lo, hi, rest, c, lap, new, nlo, nhi, pad):
    fill_pad(src, pad)
    base = block_base()
    for x in range(CX):
        curve = laplacian(x, base, pad, lo, hi, ends)
        lap[x] = curve
        new[x] = rest[x] + c[x] * c[x] * curve
    add_source(new, cells, amps[0], base)
    send_planes(new, nlo, nhi)


def scale_kernel(c, q, u, ulo, uhi):
    for x in range(CX):
        u[x] = c[x] * c[x] * q[x]
    send_planes(u, ulo, uhi)


def residual_term(step, x, res):
    lane = lax.broadcasted_iota(jnp.int32, (TY, AZ), 1)
    at = step * CX + x
    values = res[...]
    if at:
        values = pltpu.roll(values, AZ - at, 1)
    return jnp.where(lane == 0, values, 0.0)


def adjoint_kernel(step, ends, src, lo, hi, now, old, c, res, new, u, ulo, uhi, pad):
    fill_pad(src, pad)
    for x in range(CX):
        curve = laplacian(x, block_base(), pad, lo, hi, ends)
        value = 2.0 * now[x] - old[x] + curve + residual_term(step, x, res)
        new[x] = value
        u[x] = c[x] * c[x] * value
    send_planes(u, ulo, uhi)


def middle_adjoint_kernel(ends, src, lo, hi, now, old, c, res, lap1, new, u, ulo, uhi, img, pad):
    adjoint_kernel(1, ends, src, lo, hi, now, old, c, res, new, u, ulo, uhi, pad)
    for x in range(CX):
        img[x] = new[x] * lap1[x]


def image_kernel(ends, src, lo, hi, now, old, c, res, part, lap0, pair, u, ulo, uhi, img, pad):
    new = pair.at[0]
    adjoint_kernel(2, ends, src, lo, hi, now, old, c, res, new, u, ulo, uhi, pad)
    for x in range(CX):
        img[x] = part[x] + new[x] * lap0[x]


def last_adjoint_kernel(ends, src, lo, hi, now, old, res, pair, pad):
    fill_pad(src, pad)
    for x in range(CX):
        curve = laplacian(x, block_base(), pad, lo, hi, ends)
        pair[0, x] = 2.0 * now[0, x] - old[x] + curve + residual_term(3, x, res)


def forward_kernel(step, ends, cells, amps, src, lo, hi, old, c, lap, new, nlo, nhi, pad):
    fill_pad(src, pad)
    base = block_base()
    for x in range(CX):
        curve = laplacian(x, base, pad, lo, hi, ends)
        lap[x] = curve
        new[x] = 2.0 * centre(x, base, pad) - old[x] + c[x] * c[x] * curve
    add_source(new, cells, amps[step], base)
    send_planes(new, nlo, nhi)


def third_forward_kernel(
    ends, cells, amps, src, lo, hi, old, c, q3, part, img, pair, nlo, nhi, pad
):
    new = pair.at[0]
    forward_kernel(2, ends, cells, amps, src, lo, hi, old, c, img, new, nlo, nhi, pad)
    for x in range(CX):
        img[x] = part[x] + q3[x] * img[x]


def last_forward_kernel(ends, cells, amps, src, lo, hi, old, c, q4, img, pair, grad, pad):
    fill_pad(src.at[0], pad)
    new = pair.at[0]
    base = block_base()
    for x in range(CX):
        curve = laplacian(x, base, pad, lo, hi, ends)
        new[x] = 2.0 * centre(x, base, pad) - old[x] + c[x] * c[x] * curve
        grad[x] = 2.0 * c[x] * (img[x] + q4[x] * curve)
    add_source(new, cells, amps[3], base)


PAD_SCRATCH = pltpu.VMEM((CX, AY + 2 * PAD, AZ), F32)
OUTS = {
    "s": (SLAB, BLOCK),
    "h": (HALO, HBLOCK),
    "0": (PAIR, PAIR0),
    "1": (PAIR, PAIR1),
}


def size_of(shape):
    total = 4
    for n in shape:
        total *= n
    return total


def run(kernel, scalars, args, in_specs, outs, stencil=True, flops=10_000_000, aliases=None):
    kinds = [OUTS[k] for k in outs]
    traffic = sum(size_of(a.shape) for a in args) + sum(size_of(s) for s, _ in kinds)
    return pl.pallas_call(
        kernel,
        grid_spec=pltpu.PrefetchScalarGridSpec(
            num_scalar_prefetch=len(scalars),
            grid=(KY,),
            in_specs=in_specs,
            out_specs=[b for _, b in kinds],
            scratch_shapes=[PAD_SCRATCH] if stencil else [],
        ),
        out_shape=[sds(s) for s, _ in kinds],
        input_output_aliases=aliases or {},
        compiler_params=pltpu.CompilerParams(vmem_limit_bytes=VMEM),
        cost_estimate=pl.CostEstimate(flops=flops, bytes_accessed=traffic, transcendentals=0),
    )(*scalars, *args)


STENCIL = [WHOLE, HBLOCK, HBLOCK]


IN_VMEM = pl.BlockSpec(memory_space=pltpu.VMEM)
IN_SMEM = pl.BlockSpec(memory_space=pltpu.SMEM)


def pick_kernel(which, slot, b0, b1, b2, b3, out):
    for i in range(KY):
        for b, ref in enumerate((b0, b1, b2, b3)):

            @pl.when(which[i] == b)
            def _():
                out[:, i * TY : (i + 1) * TY, :] = ref[slot[i]]


def pick_tiles(which, slot, bufs):
    return pl.pallas_call(
        pick_kernel,
        in_specs=[IN_SMEM] * 2 + [IN_VMEM] * 4,
        out_specs=IN_VMEM,
        out_shape=sds(SLAB),
        compiler_params=pltpu.CompilerParams(vmem_limit_bytes=VMEM),
    )(which, slot, *bufs)


def pack_kernel(tile_of, slab, *outs):
    for b, out in enumerate(outs, 1):
        for k in range(SHARE):
            start = pl.multiple_of(tile_of[b * SHARE + k] * TY, TY)
            out[k] = slab[:, pl.ds(start, TY), :]


def pack_tiles(tile_of, slab):
    return pl.pallas_call(
        pack_kernel,
        in_specs=[IN_SMEM, IN_VMEM],
        out_specs=[IN_VMEM] * 3,
        out_shape=[sds((SHARE, CX, TY, AZ))] * 3,
        compiler_params=pltpu.CompilerParams(vmem_limit_bytes=VMEM),
    )(tile_of, slab)


def merge_kernel(used, tile_of, slab, b1, b2, b3, out):
    for slot in range(SHARE):
        start = pl.multiple_of(tile_of[slot] * TY, TY)
        for side in range(2):
            use = [used[(b * SHARE + slot) * 2 + side] == 1 for b in range(N_SHOT)]
            for x in range(CX):
                total = jnp.where(use[0], slab[x, pl.ds(start, TY), :], 0.0)
                for b, ref in enumerate((b1, b2, b3), 1):
                    total = total + jnp.where(use[b], ref[slot, x], 0.0)
                out[side * SHARE + slot, x] = total


def merge_tiles(used, tile_of, slab, bufs):
    return pl.pallas_call(
        merge_kernel,
        in_specs=[IN_SMEM] * 2 + [IN_VMEM] * 4,
        out_specs=IN_VMEM,
        out_shape=sds((2 * SHARE, CX, TY, AZ)),
        compiler_params=pltpu.CompilerParams(vmem_limit_bytes=VMEM),
    )(used, tile_of, slab, *bufs)


def within_shots(value, flip):
    return lax.ppermute(value, "shot", [(s, s ^ flip) for s in range(N_SHOT)])


def shift_column(value, amount, sign):
    def moved(value, steps):
        return lax.ppermute(value, "sub", [(j, (j + steps) % N_SUB) for j in range(N_SUB)])

    branches = [lambda v: v]
    for k in range(1, N_SUB):
        branches.append(functools.partial(moved, steps=sign * k))
    return lax.switch(amount, branches, value)


def exchange(low_planes, high_planes):
    up = [(i, (i + 1) % N_SUB) for i in range(N_SUB)]
    down = [(i, (i - 1) % N_SUB) for i in range(N_SUB)]
    before = lax.ppermute(high_planes, "sub", up)
    after = lax.ppermute(low_planes, "sub", down)
    return before, after


def body(
    courant_tiles,
    tile_place,
    anchors,
    source_cells,
    wavelet,
    forward_state,
    adjoint_state,
    residual,
):
    my_shot = lax.axis_index("shot")
    my_sub = lax.axis_index("sub")
    start_x = anchors[:, 0]
    start_y = anchors[:, 1]
    amounts = start_x % N_SUB
    upper = (my_sub < start_x).astype(jnp.int32)
    column = my_sub + upper * N_SUB
    ids = start_y[:, None] + jnp.arange(KY, dtype=jnp.int32)[None, :]
    places = tile_place[column[:, None], ids]
    own_places = places[my_shot]

    pm, p0 = forward_state[0, 0], forward_state[0, 1]
    q5, q4 = adjoint_state[0, 0], adjoint_state[0, 1]

    mine = [
        lax.dynamic_slice_in_dim(courant_tiles, upper[my_shot ^ flip] * SHARE, SHARE, 0)
        for flip in range(N_SHOT)
    ]
    bufs = [mine[0]] + [within_shots(mine[flip], flip) for flip in range(1, N_SHOT)]
    which = (own_places // SHARE) ^ my_shot
    slot = own_places % SHARE
    amount = amounts[my_shot]
    cells = source_cells[my_shot] - jnp.stack([my_sub * CX, 0, 0]).astype(jnp.int32)
    amps = wavelet[0]
    ends = jnp.stack([my_sub == 0, my_sub == N_SUB - 1]).astype(jnp.int32)
    source = (ends, cells, amps)
    res = jnp.pad(
        residual[0].reshape(STEPS * CX, AY).T, ((0, 0), (0, AZ - STEPS * CX))
    )

    (rest,) = run(rest_kernel, (), (p0, pm), [BLOCK] * 2, "s", stencil=False)
    *bufs, rest = lax.optimization_barrier((*bufs, rest))
    c = shift_column(pick_tiles(which, slot, bufs), amount, -1)
    c, low, high = lax.optimization_barrier((c, p0[0:R], p0[CX - R :]))
    before, after = exchange(low, high)
    u, ulo, uhi = run(scale_kernel, (), (c, q4), [BLOCK] * 2, "shh", stencil=False)
    ub, ua = exchange(ulo, uhi)
    lap0, p1, plo, phi = run(
        first_forward_kernel,
        source,
        (p0, before, after, rest, c),
        STENCIL + [BLOCK] * 2,
        "sshh",
    )
    pb, pa = exchange(plo, phi)
    q3, u, ulo, uhi = run(
        functools.partial(adjoint_kernel, 0),
        (ends,),
        (u, ub, ua, q4, q5, c, res),
        STENCIL + [BLOCK] * 3 + [RES],
        "sshh",
    )
    ub, ua = exchange(ulo, uhi)
    lap1, p2, plo, phi = run(
        functools.partial(forward_kernel, 1),
        source,
        (p1, pb, pa, p0, c),
        STENCIL + [BLOCK] * 2,
        "sshh",
    )
    pb, pa = exchange(plo, phi)
    q2, u, ulo, uhi, img = run(
        middle_adjoint_kernel,
        (ends,),
        (u, ub, ua, q3, q4, c, res, lap1),
        STENCIL + [BLOCK] * 3 + [RES, BLOCK],
        "sshhs",
    )
    ub, ua = exchange(ulo, uhi)
    img, forward_out, plo, phi = run(
        third_forward_kernel,
        source,
        (p2, pb, pa, p1, c, q3, img),
        STENCIL + [BLOCK] * 4,
        "s0hh",
    )
    pb, pa = exchange(plo, phi)
    adjoint_out, u, ulo, uhi, img = run(
        image_kernel,
        (ends,),
        (u, ub, ua, q2, q3, c, res, img, lap0),
        STENCIL + [BLOCK] * 3 + [RES] + [BLOCK] * 2,
        "0shhs",
    )
    ub, ua = exchange(ulo, uhi)

    holder = jnp.arange(N_SHOT, dtype=jnp.int32)[:, None] ^ my_shot
    spot = holder * SHARE + jnp.arange(SHARE, dtype=jnp.int32)[None, :]
    match = spot.reshape(-1)[:, None] == own_places[None, :]
    tile_of = jnp.sum(
        jnp.where(match, jnp.arange(KY, dtype=jnp.int32)[None, :], 0), axis=1, dtype=jnp.int32
    )
    forward_out, grad = run(
        last_forward_kernel,
        source,
        (forward_out, pb, pa, p2, c, q4, img),
        [PAIR0_WHOLE, HBLOCK, HBLOCK] + [BLOCK] * 4,
        "1s",
        aliases={3: 0},
    )
    back = shift_column(grad, amount, 1)
    parts = pack_tiles(tile_of, back)
    got = [within_shots(part, flip) for flip, part in enumerate(parts, 1)]
    (adjoint_out,) = run(
        last_adjoint_kernel,
        (ends,),
        (u, ub, ua, adjoint_out, q2, res),
        STENCIL + [PAIR0, BLOCK, RES],
        "1",
        aliases={4: 0},
    )
    *got, adjoint_out = lax.optimization_barrier((*got, adjoint_out))
    shots = jnp.arange(N_SHOT, dtype=jnp.int32) ^ my_shot
    mine = my_shot * SHARE + jnp.arange(SHARE, dtype=jnp.int32)
    covered = jnp.any(places[shots][:, None, :] == mine[None, :, None], axis=2)
    side = upper[shots][:, None, None] == jnp.arange(2, dtype=jnp.int32)[None, None, :]
    used = (covered[:, :, None] & side).astype(jnp.int32).reshape(-1)
    gradient_tiles = merge_tiles(used, tile_of[:SHARE], back, got)

    return forward_out[None], adjoint_out[None], gradient_tiles


def solution(mesh):
    return jax.shard_map(
        body,
        mesh=mesh,
        in_specs=(
            P(("shot", "sub"), None, None, None),
            P(),
            P(),
            P(),
            P("shot", None),
            P("shot", None, "sub", None, None),
            P("shot", None, "sub", None, None),
            P("shot", None, "sub", None),
        ),
        out_specs=(
            P("shot", None, "sub", None, None),
            P("shot", None, "sub", None, None),
            P(("shot", "sub"), None, None, None),
        ),
        check_vma=False,
    )
```

```python
import functools

import jax
import jax.numpy as jnp
from jax import lax
from jax.experimental import pallas as pl
from jax.experimental.pallas import tpu as pltpu
from jax.sharding import PartitionSpec as P

CX = 6
TY = 64
AZ = 128
KY = 6
AY = KY * TY
STEPS = 4
N_SHOT = 4
N_SUB = 32
SHARE = 3
R = 4
PAD = 8

WEIGHTS = (1.6, -0.2, 8.0 / 315.0, -1.0 / 560.0)
CENTER = -205.0 / 72.0 * 3.0

F32 = jnp.float32
SLAB = (CX, AY, AZ)
HALO = (R, AY, AZ)
PAIR = (2, CX, AY, AZ)
BLOCK = pl.BlockSpec((CX, TY, AZ), lambda i, *_: (0, i, 0))
HBLOCK = pl.BlockSpec((R, TY, AZ), lambda i, *_: (0, i, 0))
WHOLE = pl.BlockSpec(SLAB, lambda i, *_: (0, 0, 0))
PAIR0 = pl.BlockSpec((1, CX, TY, AZ), lambda i, *_: (0, 0, i, 0))
PAIR1 = pl.BlockSpec((1, CX, TY, AZ), lambda i, *_: (1, 0, i, 0))
PAIR0_WHOLE = pl.BlockSpec((1, CX, AY, AZ), lambda i, *_: (0, 0, 0, 0))
RES = pl.BlockSpec((TY, AZ), lambda i, *_: (i, 0))
VMEM = 20 * 1024 * 1024


def sds(shape):
    return jax.ShapeDtypeStruct(shape, F32)


def fill_pad(src, pad):
    @pl.when(pl.program_id(0) == 0)
    def _():
        pad[:, 0:PAD, :] = jnp.zeros((CX, PAD, AZ), F32)
        pad[:, PAD + AY :, :] = jnp.zeros((CX, PAD, AZ), F32)
        pad[:, PAD : PAD + AY, :] = src[...]


def centre(x, base, pad):
    return pad[x, pl.ds(base + PAD, TY), :]


def laplacian(x, base, pad, lo, hi, ends):
    def plane(k):
        if k < 0:
            return jnp.where(ends[0] == 1, 0.0, lo[k + R])
        if k >= CX:
            return jnp.where(ends[1] == 1, 0.0, hi[k - CX])
        return centre(k, base, pad)

    here = plane(x)
    lane = lax.broadcasted_iota(jnp.int32, (TY, AZ), 1)
    out = CENTER * here
    for r, w in enumerate(WEIGHTS, 1):
        out = out + w * (plane(x + r) + plane(x - r))
    for r, w in enumerate(WEIGHTS, 1):
        out = out + w * (
            pad[x, pl.ds(base + (PAD + r), TY), :] + pad[x, pl.ds(base + (PAD - r), TY), :]
        )
    for r, w in enumerate(WEIGHTS, 1):
        up = jnp.where(lane < AZ - r, pltpu.roll(here, AZ - r, 1), 0.0)
        down = jnp.where(lane >= r, pltpu.roll(here, r, 1), 0.0)
        out = out + w * (up + down)
    return out


def add_source(out, cells, amp, base):
    col = cells[1] - base
    inside = (cells[0] >= 0) & (cells[0] < CX) & (col >= 0) & (col < TY)

    @pl.when(inside)
    def _():
        lane = lax.broadcasted_iota(jnp.int32, (1, 1, AZ), 2)
        x = cells[0]
        row = out[pl.ds(x, 1), pl.ds(col, 1), :]
        out[pl.ds(x, 1), pl.ds(col, 1), :] = row + jnp.where(lane == cells[2], amp, 0.0)


def send_planes(value, lo, hi):
    lo[...] = value[0:R]
    hi[...] = value[CX - R :]


def block_base():
    return pl.multiple_of(pl.program_id(0) * TY, TY)


def scale_kernel(c, q, u, ulo, uhi):
    for x in range(CX):
        u[x] = c[x] * c[x] * q[x]
    send_planes(u, ulo, uhi)


def residual_term(step, x, res):
    lane = lax.broadcasted_iota(jnp.int32, (TY, AZ), 1)
    at = step * CX + x
    values = res[...]
    if at:
        values = pltpu.roll(values, AZ - at, 1)
    return jnp.where(lane == 0, values, 0.0)


def adjoint_kernel(step, ends, src, lo, hi, now, old, c, res, new, u, ulo, uhi, pad):
    fill_pad(src, pad)
    for x in range(CX):
        curve = laplacian(x, block_base(), pad, lo, hi, ends)
        value = 2.0 * now[x] - old[x] + curve + residual_term(step, x, res)
        new[x] = value
        u[x] = c[x] * c[x] * value
    send_planes(u, ulo, uhi)


def middle_adjoint_kernel(ends, src, lo, hi, now, old, c, res, lap1, new, u, ulo, uhi, img, pad):
    adjoint_kernel(1, ends, src, lo, hi, now, old, c, res, new, u, ulo, uhi, pad)
    for x in range(CX):
        img[x] = new[x] * lap1[x]


def image_kernel(ends, src, lo, hi, now, old, c, res, part, lap0, pair, u, ulo, uhi, img, pad):
    new = pair.at[0]
    adjoint_kernel(2, ends, src, lo, hi, now, old, c, res, new, u, ulo, uhi, pad)
    for x in range(CX):
        img[x] = part[x] + new[x] * lap0[x]


def last_adjoint_kernel(ends, src, lo, hi, now, old, res, pair, pad):
    fill_pad(src, pad)
    for x in range(CX):
        curve = laplacian(x, block_base(), pad, lo, hi, ends)
        pair[0, x] = 2.0 * now[0, x] - old[x] + curve + residual_term(3, x, res)


def forward_kernel(step, ends, cells, amps, src, lo, hi, old, c, lap, new, nlo, nhi, pad):
    fill_pad(src, pad)
    base = block_base()
    for x in range(CX):
        curve = laplacian(x, base, pad, lo, hi, ends)
        lap[x] = curve
        new[x] = 2.0 * centre(x, base, pad) - old[x] + c[x] * c[x] * curve
    add_source(new, cells, amps[step], base)
    send_planes(new, nlo, nhi)


def third_forward_kernel(
    ends, cells, amps, src, lo, hi, old, c, q3, part, img, pair, nlo, nhi, pad
):
    new = pair.at[0]
    forward_kernel(2, ends, cells, amps, src, lo, hi, old, c, img, new, nlo, nhi, pad)
    for x in range(CX):
        img[x] = part[x] + q3[x] * img[x]


def last_forward_kernel(ends, cells, amps, src, lo, hi, old, c, q4, img, pair, grad, pad):
    fill_pad(src.at[0], pad)
    new = pair.at[0]
    base = block_base()
    for x in range(CX):
        curve = laplacian(x, base, pad, lo, hi, ends)
        new[x] = 2.0 * centre(x, base, pad) - old[x] + c[x] * c[x] * curve
        grad[x] = 2.0 * c[x] * (img[x] + q4[x] * curve)
    add_source(new, cells, amps[3], base)


PAD_SCRATCH = pltpu.VMEM((CX, AY + 2 * PAD, AZ), F32)
OUTS = {
    "s": (SLAB, BLOCK),
    "h": (HALO, HBLOCK),
    "0": (PAIR, PAIR0),
    "1": (PAIR, PAIR1),
}


def size_of(shape):
    total = 4
    for n in shape:
        total *= n
    return total


def run(kernel, scalars, args, in_specs, outs, stencil=True, flops=10_000_000, aliases=None):
    kinds = [OUTS[k] for k in outs]
    traffic = sum(size_of(a.shape) for a in args) + sum(size_of(s) for s, _ in kinds)
    return pl.pallas_call(
        kernel,
        grid_spec=pltpu.PrefetchScalarGridSpec(
            num_scalar_prefetch=len(scalars),
            grid=(KY,),
            in_specs=in_specs,
            out_specs=[b for _, b in kinds],
            scratch_shapes=[PAD_SCRATCH] if stencil else [],
        ),
        out_shape=[sds(s) for s, _ in kinds],
        input_output_aliases=aliases or {},
        compiler_params=pltpu.CompilerParams(vmem_limit_bytes=VMEM),
        cost_estimate=pl.CostEstimate(flops=flops, bytes_accessed=traffic, transcendentals=0),
    )(*scalars, *args)


STENCIL = [WHOLE, HBLOCK, HBLOCK]


IN_VMEM = pl.BlockSpec(memory_space=pltpu.VMEM)
IN_SMEM = pl.BlockSpec(memory_space=pltpu.SMEM)


def pick_kernel(which, slot, b0, b1, b2, b3, out):
    for i in range(KY):
        for b, ref in enumerate((b0, b1, b2, b3)):

            @pl.when(which[i] == b)
            def _():
                out[:, i * TY : (i + 1) * TY, :] = ref[slot[i]]


def pick_tiles(which, slot, bufs):
    return pl.pallas_call(
        pick_kernel,
        in_specs=[IN_SMEM] * 2 + [IN_VMEM] * 4,
        out_specs=IN_VMEM,
        out_shape=sds(SLAB),
        compiler_params=pltpu.CompilerParams(vmem_limit_bytes=VMEM),
    )(which, slot, *bufs)


def pack_kernel(tile_of, slab, *outs):
    for b, out in enumerate(outs, 1):
        for k in range(SHARE):
            start = pl.multiple_of(tile_of[b * SHARE + k] * TY, TY)
            out[k] = slab[:, pl.ds(start, TY), :]


def pack_tiles(tile_of, slab):
    return pl.pallas_call(
        pack_kernel,
        in_specs=[IN_SMEM, IN_VMEM],
        out_specs=[IN_VMEM] * 3,
        out_shape=[sds((SHARE, CX, TY, AZ))] * 3,
        compiler_params=pltpu.CompilerParams(vmem_limit_bytes=VMEM),
    )(tile_of, slab)


def merge_kernel(used, tile_of, slab, b1, b2, b3, out):
    for slot in range(SHARE):
        start = pl.multiple_of(tile_of[slot] * TY, TY)
        for side in range(2):
            use = [used[(b * SHARE + slot) * 2 + side] == 1 for b in range(N_SHOT)]
            for x in range(CX):
                total = jnp.where(use[0], slab[x, pl.ds(start, TY), :], 0.0)
                for b, ref in enumerate((b1, b2, b3), 1):
                    total = total + jnp.where(use[b], ref[slot, x], 0.0)
                out[side * SHARE + slot, x] = total


def merge_tiles(used, tile_of, slab, bufs):
    return pl.pallas_call(
        merge_kernel,
        in_specs=[IN_SMEM] * 2 + [IN_VMEM] * 4,
        out_specs=IN_VMEM,
        out_shape=sds((2 * SHARE, CX, TY, AZ)),
        compiler_params=pltpu.CompilerParams(vmem_limit_bytes=VMEM),
    )(used, tile_of, slab, *bufs)


def scaled(c, q):
    return pl.pallas_call(
        scale_kernel,
        in_specs=[IN_VMEM] * 2,
        out_specs=[IN_VMEM] * 3,
        out_shape=[sds(SLAB), sds(HALO), sds(HALO)],
        compiler_params=pltpu.CompilerParams(vmem_limit_bytes=VMEM),
    )(c, q)


def within_shots(value, flip):
    return lax.ppermute(value, "shot", [(s, s ^ flip) for s in range(N_SHOT)])


def shift_column(value, amount, sign):
    def moved(value, steps):
        return lax.ppermute(value, "sub", [(j, (j + steps) % N_SUB) for j in range(N_SUB)])

    branches = [lambda v: v]
    for k in range(1, N_SUB):
        branches.append(functools.partial(moved, steps=sign * k))
    return lax.switch(amount, branches, value)


def exchange(low_planes, high_planes):
    up = [(i, (i + 1) % N_SUB) for i in range(N_SUB)]
    down = [(i, (i - 1) % N_SUB) for i in range(N_SUB)]
    before = lax.ppermute(high_planes, "sub", up)
    after = lax.ppermute(low_planes, "sub", down)
    return before, after


def body(
    courant_tiles,
    tile_place,
    anchors,
    source_cells,
    wavelet,
    forward_state,
    adjoint_state,
    residual,
):
    my_shot = lax.axis_index("shot")
    my_sub = lax.axis_index("sub")
    start_x = anchors[:, 0]
    start_y = anchors[:, 1]
    amounts = start_x % N_SUB
    upper = (my_sub < start_x).astype(jnp.int32)
    column = my_sub + upper * N_SUB
    ids = start_y[:, None] + jnp.arange(KY, dtype=jnp.int32)[None, :]
    places = tile_place[column[:, None], ids]
    own_places = places[my_shot]

    pm, p0 = forward_state[0, 0], forward_state[0, 1]
    q5, q4 = adjoint_state[0, 0], adjoint_state[0, 1]

    mine = [
        lax.dynamic_slice_in_dim(courant_tiles, upper[my_shot ^ flip] * SHARE, SHARE, 0)
        for flip in range(N_SHOT)
    ]
    bufs = [mine[0]] + [within_shots(mine[flip], flip) for flip in range(1, N_SHOT)]
    which = (own_places // SHARE) ^ my_shot
    slot = own_places % SHARE
    amount = amounts[my_shot]
    cells = source_cells[my_shot] - jnp.stack([my_sub * CX, 0, 0]).astype(jnp.int32)
    amps = wavelet[0]
    ends = jnp.stack([my_sub == 0, my_sub == N_SUB - 1]).astype(jnp.int32)
    source = (ends, cells, amps)
    res = jnp.pad(
        residual[0].reshape(STEPS * CX, AY).T, ((0, 0), (0, AZ - STEPS * CX))
    )

    c = shift_column(pick_tiles(which, slot, bufs), amount, -1)
    c, low, high = lax.optimization_barrier((c, p0[0:R], p0[CX - R :]))
    before, after = exchange(low, high)
    u, ulo, uhi = scaled(c, q4)
    ub, ua = exchange(ulo, uhi)
    lap0, p1, plo, phi = run(
        functools.partial(forward_kernel, 0),
        source,
        (p0, before, after, pm, c),
        STENCIL + [BLOCK] * 2,
        "sshh",
    )
    pb, pa = exchange(plo, phi)
    q3, u, ulo, uhi = run(
        functools.partial(adjoint_kernel, 0),
        (ends,),
        (u, ub, ua, q4, q5, c, res),
        STENCIL + [BLOCK] * 3 + [RES],
        "sshh",
    )
    ub, ua = exchange(ulo, uhi)
    lap1, p2, plo, phi = run(
        functools.partial(forward_kernel, 1),
        source,
        (p1, pb, pa, p0, c),
        STENCIL + [BLOCK] * 2,
        "sshh",
    )
    pb, pa = exchange(plo, phi)
    q2, u, ulo, uhi, img = run(
        middle_adjoint_kernel,
        (ends,),
        (u, ub, ua, q3, q4, c, res, lap1),
        STENCIL + [BLOCK] * 3 + [RES, BLOCK],
        "sshhs",
    )
    ub, ua = exchange(ulo, uhi)
    img, forward_out, plo, phi = run(
        third_forward_kernel,
        source,
        (p2, pb, pa, p1, c, q3, img),
        STENCIL + [BLOCK] * 4,
        "s0hh",
    )
    pb, pa = exchange(plo, phi)
    adjoint_out, u, ulo, uhi, img = run(
        image_kernel,
        (ends,),
        (u, ub, ua, q2, q3, c, res, img, lap0),
        STENCIL + [BLOCK] * 3 + [RES] + [BLOCK] * 2,
        "0shhs",
    )
    ub, ua = exchange(ulo, uhi)

    holder = jnp.arange(N_SHOT, dtype=jnp.int32)[:, None] ^ my_shot
    spot = holder * SHARE + jnp.arange(SHARE, dtype=jnp.int32)[None, :]
    match = spot.reshape(-1)[:, None] == own_places[None, :]
    tile_of = jnp.sum(
        jnp.where(match, jnp.arange(KY, dtype=jnp.int32)[None, :], 0), axis=1, dtype=jnp.int32
    )
    forward_out, grad = run(
        last_forward_kernel,
        source,
        (forward_out, pb, pa, p2, c, q4, img),
        [PAIR0_WHOLE, HBLOCK, HBLOCK] + [BLOCK] * 4,
        "1s",
        aliases={3: 0},
    )
    back = shift_column(grad, amount, 1)
    parts = pack_tiles(tile_of, back)
    got = [within_shots(part, flip) for flip, part in enumerate(parts, 1)]
    (adjoint_out,) = run(
        last_adjoint_kernel,
        (ends,),
        (u, ub, ua, adjoint_out, q2, res),
        STENCIL + [PAIR0, BLOCK, RES],
        "1",
        aliases={4: 0},
    )
    *got, adjoint_out = lax.optimization_barrier((*got, adjoint_out))
    shots = jnp.arange(N_SHOT, dtype=jnp.int32) ^ my_shot
    mine = my_shot * SHARE + jnp.arange(SHARE, dtype=jnp.int32)
    covered = jnp.any(places[shots][:, None, :] == mine[None, :, None], axis=2)
    side = upper[shots][:, None, None] == jnp.arange(2, dtype=jnp.int32)[None, None, :]
    used = (covered[:, :, None] & side).astype(jnp.int32).reshape(-1)
    gradient_tiles = merge_tiles(used, tile_of[:SHARE], back, got)

    return forward_out[None], adjoint_out[None], gradient_tiles


def solution(mesh):
    return jax.shard_map(
        body,
        mesh=mesh,
        in_specs=(
            P(("shot", "sub"), None, None, None),
            P(),
            P(),
            P(),
            P("shot", None),
            P("shot", None, "sub", None, None),
            P("shot", None, "sub", None, None),
            P("shot", None, "sub", None),
        ),
        out_specs=(
            P("shot", None, "sub", None, None),
            P("shot", None, "sub", None, None),
            P(("shot", "sub"), None, None, None),
        ),
        check_vma=False,
    )
```
